256 devices in a mesh: doc: 8 (over z), ctx: 32 (over x, y, core).
Axes of the slice: x: 4, y: 4, z: 8, core: 2. Of those that a mesh axis runs over, the one named last changes fastest.
Arguments:
- queries: bfloat16 [32768, 2048], P(('doc', 'ctx')), parts along dimension 0, may hold values from -8 to 8
- keys: bfloat16 [32768, 2048], P(('doc', 'ctx')), parts along dimension 0, may hold values from -8 to 8
- values: bfloat16 [32768, 2048], P(('doc', 'ctx')), parts along dimension 0, may hold values from -6 to 6
- out_grad: bfloat16 [32768, 2048], P(('doc', 'ctx')), parts along dimension 0, may hold values from -6 to 6
Outputs:
- attended: bfloat16 [32768, 2048], P(('doc', 'ctx')), parts along dimension 0
- query_gradient_array: bfloat16 [32768, 2048], P(('doc', 'ctx')), parts along dimension 0
- key_gradient_array: bfloat16 [32768, 2048], P(('doc', 'ctx')), parts along dimension 0
- value_gradient_array: bfloat16 [32768, 2048], P(('doc', 'ctx')), parts along dimension 0
The draws below stay inside these ranges and needn't reach their ends.
There are 8 independent parts, one for each index of `doc`. The reference program is written for one: setup_inputs(seed, part) draws one part's arguments, and reference() takes and returns one part's arrays. A program takes and returns all parts, laid end to end along the dimension named above; each array names one. Nothing has to cross between parts.
All inputs are finite; a program needn't handle non-finite values.
Results may differ from the reference program's by a relative error of at most 0.025.
The reference program's roundings to bfloat16 on the way count: a program that leaves them out, or rounds other values in their place, can miss the bound.
Values may be sent and summed in bfloat16 or wider, within the bound.
A program may use at most 128 MiB of HBM per device.

```python
import jax
import jax.numpy as jnp
from jax import lax

H = 16
DH = 128
M = 64
ITERS = 6
TOKENS = 4096
SEG = 64


def spread_rows(per_segment):
    return jnp.repeat(per_segment, TOKENS // M, axis=0, total_repeat_length=TOKENS)


def topical_rows(key):
    first, second = jax.random.split(key)
    topic = jax.random.normal(first, (M, H * DH), jnp.float32)
    noise = jax.random.normal(second, (TOKENS, H * DH), jnp.float32)
    total = spread_rows(topic) + noise
    return jnp.clip(total, -8.0, 8.0)


def draw_queries(key, part):
    key = jax.random.fold_in(key, 7)
    return topical_rows(key).astype(jnp.bfloat16)


def draw_keys(key, part):
    key = jax.random.fold_in(key, 9)
    rows = topical_rows(key)
    return rows.astype(jnp.bfloat16)


def shard_levels(key, shape, shards, least, largest):
    def one(axis_at, parts):
        heights = jax.random.uniform(jax.random.fold_in(jax.random.fold_in(key, 6), axis_at), (parts,), jnp.float32, least / len(shards), largest / len(shards))
        return jnp.repeat(jnp.exp(heights), shape[axis_at] // parts).reshape((-1,) + (1,) * (len(shape) - axis_at - 1))

    level = one(*shards[0])
    for cut in shards[1:]:
        level = level * one(*cut)
    return level


def gaussian(rng, dims, scale, reach, cuts=(), kind=jnp.bfloat16):
    gain = shard_levels(rng, dims, cuts, -0.22, 0.18) if cuts else 1.0
    values = jax.random.normal(rng, dims, jnp.float32) * scale * gain
    return jnp.minimum(jnp.maximum(values, -reach), reach).astype(kind)


def setup_inputs(seed: int = 0, part: int = 0) -> dict:
    seeds = jax.random.split(jax.random.key(seed), 5)
    part_keys = jax.random.split(jax.random.fold_in(seeds[4], part), 5)
    queries = draw_queries(jax.random.fold_in(jax.random.fold_in(seeds[4], part), 71), part)
    keys = draw_keys(jax.random.fold_in(jax.random.fold_in(seeds[4], part), 71), part)
    values = gaussian(part_keys[2], (TOKENS, H * DH), 1.0, 6.0, ((0, 32),))
    out_grad = gaussian(part_keys[3], (TOKENS, H * DH), 1.0, 6.0, ((0, 32),))
    return dict(queries=queries, keys=keys, values=values, out_grad=out_grad)


def softmax_final_axis(scores):
    maxima = lax.optimization_barrier(jnp.max(scores, axis=-1, keepdims=True))
    expos = jnp.exp(scores - maxima)
    return expos / lax.optimization_barrier(jnp.sum(expos, axis=-1, keepdims=True))

def batch_product(left, right):
    return jnp.einsum('hij,hjk->hik', left, right, precision=lax.Precision.HIGHEST)

def newton_inverse(amat):
    count = amat.shape[-1]
    colmax = lax.optimization_barrier(jnp.max(lax.optimization_barrier(jnp.sum(amat, axis=1)), axis=-1))
    rowmax = lax.optimization_barrier(jnp.max(lax.optimization_barrier(jnp.sum(amat, axis=2)), axis=-1))
    divisor = lax.stop_gradient(colmax * rowmax)
    approx = jnp.swapaxes(amat, 1, 2) / divisor[:, None, None]
    unit_matrix = jnp.eye(count, dtype=amat.dtype)
    for sweep in range(ITERS):
        product = batch_product(amat, approx)
        middle = 7.0 * unit_matrix - product
        middle = 15.0 * unit_matrix - batch_product(product, middle)
        middle = 13.0 * unit_matrix - batch_product(product, middle)
        approx = 0.25 * batch_product(approx, middle)
    return approx

def broad_result(array):
    return array.astype(jnp.float32)

def reference(queries, keys, values, out_grad):
    running_highest = lax.Precision.HIGHEST
    total_rows = queries.shape[0]
    scale_factor = DH ** (-0.5)
    query_per_head = queries.reshape(total_rows, H, DH)
    key_per_head = keys.reshape(total_rows, H, DH)
    value_per_head = values.reshape(total_rows, H, DH)
    output_gradient_heads = out_grad.reshape(total_rows, H, DH)
    landmark_query_rows = lax.optimization_barrier(jnp.mean(broad_result(query_per_head).reshape(M, SEG, H, DH), axis=1)).astype(jnp.bfloat16)
    landmark_key_rows = lax.optimization_barrier(jnp.mean(broad_result(key_per_head).reshape(M, SEG, H, DH), axis=1)).astype(jnp.bfloat16)
    left_kernel_probs = softmax_final_axis(jnp.einsum('ylu,blu->lyb', broad_result(query_per_head), broad_result(landmark_key_rows), precision=running_highest) * scale_factor)
    left_kernel_reduced = left_kernel_probs.astype(jnp.bfloat16)
    a_prob = softmax_final_axis(jnp.einsum('ihd,jhd->hij', broad_result(landmark_query_rows), broad_result(landmark_key_rows), precision=running_highest) * scale_factor)
    middle_kernel_probs = softmax_final_axis(jnp.einsum('spe,bpe->psb', broad_result(landmark_query_rows), broad_result(key_per_head), precision=running_highest) * scale_factor)
    right_kernel_matrix = jnp.einsum('ioq,qif->iof', middle_kernel_probs, broad_result(value_per_head), precision=running_highest)
    pseudo_inverse_matrix, newton_back = jax.vjp(newton_inverse, a_prob)
    context_reduced = batch_product(pseudo_inverse_matrix, right_kernel_matrix).astype(jnp.bfloat16)
    attended = jnp.einsum('pbk,pkj->bpj', broad_result(left_kernel_reduced), broad_result(context_reduced), precision=running_highest).astype(jnp.bfloat16)
    left_kernel_gradient = jnp.einsum('oge,gye->goy', broad_result(output_gradient_heads), broad_result(context_reduced), precision=running_highest)
    context_gradient = jnp.einsum('spx,pst->sxt', broad_result(left_kernel_reduced), broad_result(output_gradient_heads), precision=running_highest)
    pseudo_inverse_gradient = jnp.einsum('uqg,usg->uqs', context_gradient, right_kernel_matrix, precision=running_highest)
    right_kernel_gradient = jnp.einsum('gwn,gwe->gne', pseudo_inverse_matrix, context_gradient, precision=running_highest)
    a_grad, = newton_back(pseudo_inverse_gradient)
    right_kernel_reduced = right_kernel_gradient.astype(jnp.bfloat16)
    middle_kernel_gradient = jnp.einsum('wcv,swv->wcs', broad_result(right_kernel_reduced), broad_result(value_per_head), precision=running_highest)
    b_dot = lax.optimization_barrier(jnp.sum(middle_kernel_probs * middle_kernel_gradient, axis=-1, keepdims=True))
    middle_kernel_logits = (middle_kernel_probs * (middle_kernel_gradient - b_dot)).astype(jnp.bfloat16)
    value_gradient_array = jnp.einsum('tye,tyc->etc', broad_result(middle_kernel_probs.astype(jnp.bfloat16)), broad_result(right_kernel_reduced), precision=running_highest).astype(jnp.bfloat16)
    left_kernel_logits = (left_kernel_probs * (left_kernel_gradient - lax.optimization_barrier(jnp.sum(left_kernel_probs * left_kernel_gradient, axis=-1, keepdims=True)))).astype(jnp.bfloat16)
    a_score = a_prob * (a_grad - lax.optimization_barrier(jnp.sum(a_prob * a_grad, axis=-1, keepdims=True)))
    query_landmark_gradient = jnp.einsum('gab,bgo->ago', broad_result(middle_kernel_logits), broad_result(key_per_head), precision=running_highest) * scale_factor
    query_landmark_gradient = query_landmark_gradient + jnp.einsum('hij,jhd->ihd', a_score, broad_result(landmark_key_rows), precision=running_highest) * scale_factor
    key_landmark_gradient = jnp.einsum('ksi,ska->ika', broad_result(left_kernel_logits), broad_result(query_per_head), precision=running_highest) * scale_factor
    key_landmark_gradient = key_landmark_gradient + jnp.einsum('hij,ihd->jhd', a_score, broad_result(landmark_query_rows), precision=running_highest) * scale_factor
    query_gradient_array = jnp.einsum('spg,gsu->psu', broad_result(left_kernel_logits), broad_result(landmark_key_rows), precision=running_highest) * scale_factor
    query_gradient_array = query_gradient_array + jnp.repeat(query_landmark_gradient / SEG, SEG, axis=0)
    key_gradient_array = jnp.einsum('zlk,lzw->kzw', broad_result(middle_kernel_logits), broad_result(landmark_query_rows), precision=running_highest) * scale_factor
    key_gradient_array = key_gradient_array + jnp.repeat(key_landmark_gradient / SEG, SEG, axis=0)
    width = H * DH
    return (attended.reshape(total_rows, width), query_gradient_array.astype(jnp.bfloat16).reshape(total_rows, width), key_gradient_array.astype(jnp.bfloat16).reshape(total_rows, width), value_gradient_array.reshape(total_rows, width))
```

```python
import jax
import jax.numpy as jnp
from jax import lax
from jax.experimental import pallas as pl
from jax.experimental.pallas import tpu as pltpu
from jax.sharding import PartitionSpec as P

H = 16
DH = 128
M = 64
ITERS = 6
SCALE = DH ** (-0.5)
MESH = pl.DeviceIdType.MESH
HIGHEST = lax.Precision.HIGHEST
BF = jnp.bfloat16
F32 = jnp.float32
NX, NY, NC = 4, 4, 2
CHIPS = NX * NY
GROUP = CHIPS * NC
ROWS = 128
SEG = 64
WIDTH = H * DH
MSG = 72

OFFSETS = [
    (dx, dy, dc)
    for dx in (2, 1, 3, 0)
    for dy in (2, 1, 3, 0)
    for dc in (0, 1)
    if (dx, dy, dc) != (0, 0, 0)
]


def nn(a, b, precision=None):
    return lax.dot_general(
        a, b, (((1,), (0,)), ((), ())), precision=precision, preferred_element_type=F32
    )


def nt(a, b, precision=None):
    return lax.dot_general(
        a, b, (((1,), (1,)), ((), ())), precision=precision, preferred_element_type=F32
    )


def tn(a, b, precision=None):
    return lax.dot_general(
        a, b, (((0,), (0,)), ((), ())), precision=precision, preferred_element_type=F32
    )


def iota(shape, dim):
    return lax.broadcasted_iota(jnp.int32, shape, dim)


def wait_bytes(ref, sem):
    pltpu.make_async_copy(ref, ref, sem).wait()


def head_cols(h):
    return pl.ds(pl.multiple_of(h * DH, DH), DH)


def kernel(
    q_hbm, k_hbm, v_hbm, g_hbm,
    att_hbm, qg_hbm, kg_hbm, vg_hbm,
    q_v, k_v, v_v, g_v,
    msg32, msg16, rb, lf, ql, kl,
    f_s, w_s, m_s, part, inbox, comb, fin,
    res, stat, cmat_in, cmat_out, ab, sb,
    s32, s16, r4, fs_s, bs_s, bl_s, asc_s,
    att_v, vg_v, qg32, kg32, qg_v, kg_v,
    in_sem, out_sem, e1_s, e1_r, sw_s, sw_r, e2_s, e2_r,
    cm_s, cm_r, e3_s, e3_r, e3t_s, e3t_r, e4_s, e4_r,
):
    me = lax.axis_index("ctx")
    core = lax.rem(me, NC)
    chip = me // NC
    y = lax.rem(chip, NY)
    x = chip // NY

    def peer(offset):
        dx, dy, dc = offset
        return (
            (lax.rem(x + dx, NX) * NY + lax.rem(y + dy, NY)) * NC + lax.rem(core + dc, NC)
        )

    partner = chip * NC + (1 - core)

    def remote(src, dst, send, recv, target):
        return pltpu.make_async_remote_copy(
            src_ref=src, dst_ref=dst, send_sem=send, recv_sem=recv,
            device_id={"ctx": target}, device_id_type=MESH,
        )

    barrier = pltpu.get_barrier_semaphore()
    for offset in OFFSETS:
        pl.semaphore_signal(
            barrier, inc=1, device_id={"ctx": peer(offset)}, device_id_type=MESH
        )
    loads = []
    for slot, (src, dst) in enumerate(
        ((q_hbm, q_v), (k_hbm, k_v), (v_hbm, v_v), (g_hbm, g_v))
    ):
        copy = pltpu.make_async_copy(src, dst, in_sem.at[slot])
        copy.start()
        loads.append(copy)

    pick = jnp.where(iota((8, ROWS), 0) == iota((8, ROWS), 1) // SEG, 1.0, 0.0).astype(BF)
    for which, ref in ((0, q_v), (1, k_v)):
        loads[which].wait()
        sums = nn(pick, ref[...]) * (1.0 / SEG)
        for seg in range(2):
            for h in range(H):
                row = which * 32 + seg * H + h
                msg32[row : row + 1, :] = sums[seg : seg + 1, h * DH : (h + 1) * DH]
    msg16[...] = msg32[...].astype(BF)
    rb[me] = msg16[...]
    pl.semaphore_wait(barrier, GROUP - 1)
    for offset in OFFSETS:
        remote(msg16, rb.at[me], e1_s, e1_r, peer(offset)).start()
    loads[2].wait()
    loads[3].wait()
    wait_bytes(rb.at[0 : GROUP - 1], e1_r)

    for d in range(GROUP):
        for which in range(2):
            lf[which, d * 32 : (d + 1) * 32, :] = rb[d, which * 32 : (which + 1) * 32, :].astype(F32)

    row_at = iota((M, DH), 0)
    lane_at = iota((M, DH), 1)
    diag_low = lane_at == row_at
    diag_high = lane_at == row_at + M

    def landmarks(which, h):
        return lf[which, pl.ds(h, M, stride=H), :].astype(BF)

    def to_col(row):
        return jnp.sum(jnp.where(diag_low, row, 0.0), axis=1, keepdims=True)

    m_s[...] = jnp.zeros_like(m_s)

    def local_group(heads):
        kls, qls, sfs, sbs = [], [], [], []
        for h in heads:
            kl_h = landmarks(1, h)
            ql_h = landmarks(0, h)
            kls.append(kl_h)
            qls.append(ql_h)
            sfs.append(nt(kl_h, q_v[:, head_cols(h)]) * SCALE)
            sbs.append(nt(ql_h, k_v[:, head_cols(h)]) * SCALE)
        fps, gps = [], []
        for h, sf in zip(heads, sfs):
            e = jnp.exp(sf - jnp.max(sf, axis=0, keepdims=True))
            fp = e / jnp.sum(e, axis=0, keepdims=True)
            fps.append(fp)
            gps.append(nn(fp.astype(BF), g_v[:, head_cols(h)]))
        ws, cps, rows, ms = [], [], [], []
        for h, s in zip(heads, sbs):
            m = jnp.max(s, axis=1, keepdims=True)
            w = jnp.exp(s - m)
            t = jnp.sum(w, axis=1, keepdims=True)
            hi = w.astype(BF)
            lo = (w - hi.astype(F32)).astype(BF)
            vals = v_v[:, head_cols(h)]
            cps.append(nn(hi, vals) + nn(lo, vals))
            rows.append(
                jnp.sum(
                    jnp.where(diag_low, m, 0.0) + jnp.where(diag_high, t, 0.0),
                    axis=0, keepdims=True,
                )
            )
            ws.append(w)
            ms.append(m)
        known = m_s[...]
        for h, m in zip(heads, ms):
            known = jnp.where(lane_at == h, m, known)
        m_s[...] = known
        for j, h in enumerate(heads):
            kl[h] = kls[j]
            ql[h] = qls[j]
            f_s[h] = fps[j]
            w_s[h] = ws[j]
            part[0, h, 0:M, :] = cps[j]
            part[0, h, M:MSG, :] = jnp.broadcast_to(rows[j], (MSG - M, DH))
            part[1, h, 0:M, :] = gps[j]
            part[1, h, M:MSG, :] = jnp.zeros((MSG - M, DH), F32)

    def combine(heads):
        out = []
        for h in heads:
            row0 = part[core, h, M : M + 1, :]
            row1 = inbox[h, M : M + 1, :]
            top = jnp.maximum(row0, row1)
            f0 = jnp.exp(row0 - top)
            f1 = jnp.exp(row1 - top)
            t = pltpu.roll(f0, M, 1) * row0 + pltpu.roll(f1, M, 1) * row1
            row = jnp.where(iota((1, DH), 1) < M, top, t)
            total = part[core, h, 0:M, :] * to_col(f0) + inbox[h, 0:M, :] * to_col(f1)
            out.append((total, row))
        for h, (total, row) in zip(heads, out):
            comb[h, 0:M, :] = total
            comb[h, M:MSG, :] = jnp.broadcast_to(row, (MSG - M, DH))

    def group_of(i):
        return lax.rem(x + 1 + i, NX)

    def heads_of(i):
        return [group_of(i) * NY + lax.rem(y + 1 + j, NY) for j in range(NY)]

    swaps = []

    def finish(i):
        swaps[i].wait_recv()
        heads = heads_of(i)
        combine(heads)
        for j, h in enumerate(heads):
            if i == NX - 1 and j == NY - 1:
                fin[chip] = comb[h]
            else:
                remote(comb.at[h], fin.at[chip], e2_s, e2_r, h * NC + core).start()

    for i in range(NX):
        local_group(heads_of(i))
        block = pl.ds(group_of(i) * NY, NY)
        swap = remote(
            part.at[1 - core, block], inbox.at[block], sw_s.at[i], sw_r.at[i], partner
        )
        swap.start()
        swaps.append(swap)
        if i > 0:
            finish(i - 1)
    finish(NX - 1)

    ql_own = ql[chip]
    kl_own = kl[chip]
    scores = nt(ql_own, kl_own) * SCALE
    e = jnp.exp(scores - jnp.max(scores, axis=1, keepdims=True))
    a = e / jnp.sum(e, axis=1, keepdims=True)
    divisor = jnp.max(jnp.sum(a, axis=0, keepdims=True), axis=1, keepdims=True) * jnp.max(
        jnp.sum(a, axis=1, keepdims=True), axis=0, keepdims=True
    )
    a_t = a.T
    z = a_t / divisor
    unit = jnp.where(iota((M, M), 0) == iota((M, M), 1), 1.0, 0.0)
    sweeps = []
    for _ in range(ITERS):
        p = nn(a, z, HIGHEST)
        q1 = 7.0 * unit - p
        q2 = 15.0 * unit - nn(p, q1, HIGHEST)
        q3 = 13.0 * unit - nn(p, q2, HIGHEST)
        sweeps.append((z.T, p.T, q1, q2, q3))
        z = 0.25 * nn(z, q3, HIGHEST)
    left = jnp.where(core == 0, z, z.T)

    wait_bytes(fin.at[0 : CHIPS - 1], e2_r)
    rows = jnp.concatenate([fin[s, M : M + 1, :] for s in range(CHIPS)], axis=0)
    top = jnp.max(rows, axis=0, keepdims=True)
    factor = jnp.exp(rows - top)
    total = jnp.sum(factor * pltpu.roll(rows, M, 1), axis=0, keepdims=True)
    low = iota((1, DH), 1) < M
    inverse = jnp.where(low, 1.0 / jnp.where(low & (core == 0), total, 1.0), 0.0)
    eye_low = jnp.where(diag_low, 1.0, 0.0)
    weight = nt(eye_low, factor * inverse, HIGHEST)
    summed = fin[0, 0:M, :] * weight[:, 0:1]
    for s in range(1, CHIPS):
        summed = summed + fin[s, 0:M, :] * weight[:, s : s + 1]
    made = nn(left, summed, HIGHEST).astype(BF)
    res[...] = made
    ab[me] = made
    for offset in OFFSETS:
        remote(res, ab.at[me], e3_s, e3_r, peer(offset)).start()

    def send_stat():
        sb[me] = stat[...]
        for offset in OFFSETS:
            remote(stat, sb.at[me], e3t_s, e3t_r, peer(offset)).start()

    @pl.when(core == 0)
    def _():
        cmat_out[...] = summed
        remote(cmat_out, cmat_in, cm_s, cm_r, partner).start()
        stat[...] = jnp.where(iota((8, DH), 0) == 0, top, inverse)
        send_stat()
        wait_bytes(cmat_out, cm_s)

    @pl.when(core == 1)
    def _():
        wait_bytes(cmat_in, cm_r)
        c = cmat_in[...]
        dots = jnp.sum(made.astype(F32) * c, axis=1, keepdims=True)
        stat[...] = jnp.broadcast_to(
            jnp.sum(jnp.where(diag_low, dots, 0.0), axis=0, keepdims=True), (8, DH)
        )
        send_stat()
        grad = nt(summed, c, HIGHEST)
        a_grad = jnp.zeros((M, M), F32)
        for z_t, p_t, r1, r2, r3 in sweeps[::-1]:
            d3 = 0.25 * nn(z_t, grad, HIGHEST)
            dz = 0.25 * nt(grad, r3, HIGHEST)
            d2 = -nn(p_t, d3, HIGHEST)
            dp = -nt(d3, r2, HIGHEST) - nt(d2, r1, HIGHEST) + nn(p_t, d2, HIGHEST)
            a_grad = a_grad + nn(dp, z_t, HIGHEST)
            grad = dz + nn(a_t, dp, HIGHEST)
        a_grad = a_grad + grad.T / divisor
        a_score = a * (a_grad - jnp.sum(a * a_grad, axis=1, keepdims=True))
        asc_s[0] = nn(a_score, kl_own.astype(F32), HIGHEST) * SCALE
        asc_s[1] = nn(a_score.T, ql_own.astype(F32), HIGHEST) * SCALE

    wait_bytes(ab.at[0 : GROUP - 1], e3_r)
    wait_bytes(sb.at[0 : GROUP - 1], e3t_r)

    gathered = jnp.concatenate(
        [sb[NC * h, 0:1, :] for h in range(H)]
        + [sb[NC * h, 1:2, :] for h in range(H)]
        + [sb[NC * h + 1, 0:1, :] for h in range(H)],
        axis=0,
    )
    cols = nt(eye_low, gathered, HIGHEST)
    alphas = jnp.exp(m_s[:, 0:H] - cols[:, 0:H]) * cols[:, H : 2 * H]

    for base in range(0, H, 4):
        heads = range(base, base + 4)
        fgs = [nt(ab[NC * h], g_v[:, h * DH : (h + 1) * DH]) for h in heads]
        bgs = [nt(ab[NC * h + 1], v_v[:, h * DH : (h + 1) * DH]) for h in heads]
        outs = []
        for h, fg, bg in zip(heads, fgs, bgs):
            fp = f_s[h]
            fs = (fp * (fg - jnp.sum(fp * fg, axis=0, keepdims=True))).astype(BF)
            bp = w_s[h] * alphas[:, h : h + 1]
            bs = (bp * (bg - cols[:, 2 * H + h : 2 * H + h + 1])).astype(BF)
            kp = nn(fs, q_v[:, h * DH : (h + 1) * DH]) * SCALE
            qp = nn(bs, k_v[:, h * DH : (h + 1) * DH]) * SCALE
            outs.append((fs, bs, bp.astype(BF), qp, kp))
        for h, (fs, bs, bl, qp, kp) in zip(heads, outs):
            fs_s[h] = fs
            bs_s[h] = bs
            bl_s[h] = bl
            s32[0, pl.ds(h, M, stride=H), :] = qp
            s32[1, pl.ds(h, M, stride=H), :] = kp

    @pl.when(core == 1)
    def _():
        for which in range(2):
            at = pl.ds(chip, M, stride=H)
            s32[which, at, :] = s32[which, at, :] + asc_s[which]

    for d in range(GROUP):
        for which in range(2):
            s16[d, which * 32 : (which + 1) * 32, :] = s32[which, d * 32 : (d + 1) * 32, :].astype(BF)
    r4[me] = s16[me]
    for offset in OFFSETS:
        remote(s16.at[peer(offset)], r4.at[me], e4_s, e4_r, peer(offset)).start()

    for h in range(H):
        at = slice(h * DH, (h + 1) * DH)
        att_v[:, at] = tn(f_s[h].astype(BF), ab[NC * h]).astype(BF)
        vg_v[:, at] = tn(bl_s[h], ab[NC * h + 1]).astype(BF)
    out_a = pltpu.make_async_copy(att_v, att_hbm, out_sem.at[0])
    out_v = pltpu.make_async_copy(vg_v, vg_hbm, out_sem.at[3])
    out_a.start()
    out_v.start()
    for h in range(H):
        at = slice(h * DH, (h + 1) * DH)
        qg32[:, at] = tn(fs_s[h], kl[h]) * SCALE
        kg32[:, at] = tn(bs_s[h], ql[h]) * SCALE

    wait_bytes(r4.at[0 : GROUP - 1], e4_r)
    land = r4[0].astype(F32)
    for d in range(1, GROUP):
        land = land + r4[d].astype(F32)
    land = land * (1.0 / SEG)
    for h in range(H):
        at = slice(h * DH, (h + 1) * DH)
        for seg in range(2):
            here = slice(seg * SEG, (seg + 1) * SEG)
            row = seg * H + h
            qg_v[here, at] = (qg32[here, at] + land[row : row + 1, :]).astype(BF)
            kg_v[here, at] = (kg32[here, at] + land[32 + row : 32 + row + 1, :]).astype(BF)
    out_q = pltpu.make_async_copy(qg_v, qg_hbm, out_sem.at[1])
    out_k = pltpu.make_async_copy(kg_v, kg_hbm, out_sem.at[2])
    out_q.start()
    out_k.start()

    wait_bytes(rb.at[0 : GROUP - 1], e1_s)
    for swap in swaps:
        swap.wait_send()
    wait_bytes(fin.at[0 : CHIPS - 1], e2_s)
    wait_bytes(ab.at[0 : GROUP - 1], e3_s)
    wait_bytes(sb.at[0 : GROUP - 1], e3t_s)
    wait_bytes(r4.at[0 : GROUP - 1], e4_s)
    for copy in (out_a, out_v, out_q, out_k):
        copy.wait()


def per_device(queries, keys, values, out_grad):
    shape = (ROWS, WIDTH)
    dma = pltpu.SemaphoreType.DMA
    rows = pltpu.VMEM(shape, BF)
    scratch = (
        [rows] * 4
        + [pltpu.VMEM((64, DH), F32), pltpu.VMEM((64, DH), BF)]
        + [pltpu.VMEM((GROUP, 64, DH), BF), pltpu.VMEM((2, M * H, DH), F32)]
        + [pltpu.VMEM((H, M, DH), BF)] * 2
        + [pltpu.VMEM((H, M, ROWS), F32)] * 2
        + [pltpu.VMEM((M, DH), F32)]
        + [pltpu.VMEM((2, H, MSG, DH), F32)]
        + [pltpu.VMEM((H, MSG, DH), F32)] * 3
        + [pltpu.VMEM((M, DH), BF), pltpu.VMEM((8, DH), F32)]
        + [pltpu.VMEM((M, DH), F32)] * 2
        + [pltpu.VMEM((GROUP, M, DH), BF), pltpu.VMEM((GROUP, 8, DH), F32)]
        + [pltpu.VMEM((2, M * H, DH), F32)]
        + [pltpu.VMEM((GROUP, 64, DH), BF)] * 2
        + [pltpu.VMEM((H, M, ROWS), BF)] * 3
        + [pltpu.VMEM((2, M, DH), F32)]
        + [rows] * 2
        + [pltpu.VMEM(shape, F32)] * 2
        + [rows] * 2
        + [dma((4,)), dma((4,)), dma, dma, dma((NX,)), dma((NX,))]
        + [dma] * 10
    )
    return pl.pallas_call(
        kernel,
        out_shape=[jax.ShapeDtypeStruct(shape, BF)] * 4,
        in_specs=[pl.BlockSpec(memory_space=pl.ANY)] * 4,
        out_specs=[pl.BlockSpec(memory_space=pl.ANY)] * 4,
        scratch_shapes=scratch,
        compiler_params=pltpu.CompilerParams(
            collective_id=0, has_side_effects=True, vmem_limit_bytes=56 << 20
        ),
    )(queries, keys, values, out_grad)


def solution(mesh):
    placed = P(("doc", "ctx"), None)
    return jax.shard_map(
        per_device,
        mesh=mesh,
        in_specs=(placed,) * 4,
        out_specs=(placed,) * 4,
        check_vma=False,
    )
```

```python
import jax
import jax.numpy as jnp
from jax import lax
from jax.experimental import pallas as pl
from jax.experimental.pallas import tpu as pltpu
from jax.sharding import PartitionSpec as P

H = 16
DH = 128
M = 64
ITERS = 6
SCALE = DH ** (-0.5)
MESH = pl.DeviceIdType.MESH
HIGHEST = lax.Precision.HIGHEST
BF = jnp.bfloat16
F32 = jnp.float32
NX, NY, NC = 4, 4, 2
CHIPS = NX * NY
GROUP = CHIPS * NC
ROWS = 128
SEG = 64
WIDTH = H * DH

OFFSETS = [
    (dx, dy, dc)
    for dx in (2, 1, 3, 0)
    for dy in (2, 1, 3, 0)
    for dc in (0, 1)
    if (dx, dy, dc) != (0, 0, 0)
]


STEPS = [(dx, dy) for dx, dy, dc in OFFSETS if dc == 0]


def nn(a, b, precision=None):
    return lax.dot_general(
        a, b, (((1,), (0,)), ((), ())), precision=precision, preferred_element_type=F32
    )


def nt(a, b, precision=None):
    return lax.dot_general(
        a, b, (((1,), (1,)), ((), ())), precision=precision, preferred_element_type=F32
    )


def tn(a, b, precision=None):
    return lax.dot_general(
        a, b, (((0,), (0,)), ((), ())), precision=precision, preferred_element_type=F32
    )


def iota(shape, dim):
    return lax.broadcasted_iota(jnp.int32, shape, dim)


def wait_bytes(ref, sem):
    pltpu.make_async_copy(ref, ref, sem).wait()


def head_cols(h):
    return pl.ds(pl.multiple_of(h * DH, DH), DH)


def kernel(
    q_hbm, k_hbm, v_hbm, g_hbm,
    att_v, vg_v, qg32, kg32, land,
    q_v, k_v, v_v, g_v,
    msg32, msg16, rb, lf, ql, kl,
    f_s, w_s, part, inbox, comb, fin, mt_s, mt_in, mt_c, mt_f, sum_s,
    lefts, steps, sides,
    res, stat, cmat_in, cmat_out, ab, sb,
    gpart, ginb, s32, s16, r4, fs_s, bs_s, bl_s, asc_s,
    in_sem, e1_s, e1_r, sw_s, sw_r, mt_ss, mt_sr, e2_s, e2_r, e2t_s, e2t_r,
    cm_s, cm_r, e3_s, e3_r, e3t_s, e3t_r, gs_s, gs_r, e4_s, e4_r,
):
    me = lax.axis_index("ctx")
    core = lax.rem(me, NC)
    chip = me // NC
    y = lax.rem(chip, NY)
    x = chip // NY

    def peer(offset):
        dx, dy, dc = offset
        return (
            (lax.rem(x + dx, NX) * NY + lax.rem(y + dy, NY)) * NC + lax.rem(core + dc, NC)
        )

    partner = chip * NC + (1 - core)

    def remote(src, dst, send, recv, target):
        return pltpu.make_async_remote_copy(
            src_ref=src, dst_ref=dst, send_sem=send, recv_sem=recv,
            device_id={"ctx": target}, device_id_type=MESH,
        )

    def spread(block, slots, send, recv):
        for dx, dy in STEPS:
            remote(
                block, slots.at[core, chip], send.at[NX], recv.at[dx], peer((dx, dy, 0))
            ).start()

    def relay_row(slots, send, recv, dx):
        row = lax.rem(x + NX - dx, NX) * NY
        wait_bytes(slots.at[core, pl.ds(0, NY - 1 if dx == 0 else NY)], recv.at[dx])
        block = slots.at[core, pl.ds(row, NY)]
        copy = remote(block, block, send.at[dx], recv.at[NX + dx], partner)
        copy.start()
        return copy

    def relay(slots, send, recv):
        return [relay_row(slots, send, recv, dx) for dx in (0, 1, 3, 2)]

    def settle(slots, copies, send):
        wait_bytes(slots.at[core, pl.ds(0, CHIPS - 1)], send.at[NX])
        for copy in copies:
            copy.wait_send()

    barrier = pltpu.get_barrier_semaphore()
    for offset in OFFSETS:
        pl.semaphore_signal(
            barrier, inc=1, device_id={"ctx": peer(offset)}, device_id_type=MESH
        )
    loads = []
    for slot, (src, dst) in enumerate(
        ((q_hbm, q_v), (k_hbm, k_v), (v_hbm, v_v), (g_hbm, g_v))
    ):
        copy = pltpu.make_async_copy(src, dst, in_sem.at[slot])
        copy.start()
        loads.append(copy)

    pick = jnp.where(iota((8, ROWS), 0) == iota((8, ROWS), 1) // SEG, 1.0, 0.0).astype(BF)
    for which, ref in ((0, q_v), (1, k_v)):
        loads[which].wait()
        sums = nn(pick, ref[...]) * (1.0 / SEG)
        for seg in range(2):
            for h in range(H):
                row = which * 32 + seg * H + h
                msg32[row : row + 1, :] = sums[seg : seg + 1, h * DH : (h + 1) * DH]
    msg16[...] = msg32[...].astype(BF)
    rb[core, chip] = msg16[...]
    pl.semaphore_wait(barrier, GROUP - 1)
    spread(msg16, rb, e1_s, e1_r)
    loads[2].wait()
    loads[3].wait()
    relays = relay(rb, e1_s, e1_r)
    for copy in relays:
        copy.wait_recv()

    for c in range(NC):
        for d in range(CHIPS):
            for which in range(2):
                at = (d * NC + c) * 32
                lf[which, at : at + 32, :] = rb[c, d, which * 32 : (which + 1) * 32, :].astype(F32)

    row_at = iota((M, DH), 0)
    lane_at = iota((M, DH), 1)
    diag_low = lane_at == row_at
    diag_high = lane_at == row_at + M

    def landmarks(which, h):
        return lf[which, pl.ds(h, M, stride=H), :].astype(BF)

    def to_col(row):
        return jnp.sum(jnp.where(diag_low, row, 0.0), axis=1, keepdims=True)

    low = iota((1, DH), 1) < M
    eye_low = jnp.where(diag_low, 1.0, 0.0)

    def local_group(heads):
        kls, qls, sfs, sbs = [], [], [], []
        for h in heads:
            kl_h = landmarks(1, h)
            ql_h = landmarks(0, h)
            kls.append(kl_h)
            qls.append(ql_h)
            sfs.append(nt(kl_h, q_v[:, head_cols(h)]) * SCALE)
            sbs.append(nt(ql_h, k_v[:, head_cols(h)]) * SCALE)
        fps, gps = [], []
        for h, sf in zip(heads, sfs):
            e = jnp.exp(sf - jnp.max(sf, axis=0, keepdims=True))
            fp = e / jnp.sum(e, axis=0, keepdims=True)
            fps.append(fp)
            gps.append(nn(fp.astype(BF), g_v[:, head_cols(h)]))
        ws, cps, rows = [], [], []
        for h, s in zip(heads, sbs):
            m = jnp.max(s, axis=1, keepdims=True)
            w = jnp.exp(s - m)
            t = jnp.sum(w, axis=1, keepdims=True)
            hi = w.astype(BF)
            lo = (w - hi.astype(F32)).astype(BF)
            vals = v_v[:, head_cols(h)]
            cps.append(nn(hi, vals) + nn(lo, vals))
            rows.append(
                jnp.sum(
                    jnp.where(diag_low, m, 0.0) + jnp.where(diag_high, t, 0.0),
                    axis=0, keepdims=True,
                )
            )
            ws.append(w)
        for j, h in enumerate(heads):
            kl[h] = kls[j]
            ql[h] = qls[j]
            f_s[h] = fps[j]
            w_s[h] = ws[j]
            part[0, h] = cps[j]
            part[1, h] = gps[j]
            mt_s[h] = rows[j]

    def combine(heads):
        @pl.when(core == 0)
        def _():
            out = []
            for h in heads:
                row0 = mt_s[h]
                row1 = mt_in[h]
                top = jnp.maximum(row0, row1)
                f0 = jnp.exp(row0 - top)
                f1 = jnp.exp(row1 - top)
                t = pltpu.roll(f0, M, 1) * row0 + pltpu.roll(f1, M, 1) * row1
                both = part[0, h] * to_col(f0) + inbox[h] * to_col(f1)
                out.append((both, jnp.where(low, top, t)))
            for h, (both, row) in zip(heads, out):
                comb[h] = both
                mt_c[h] = row

        @pl.when(core == 1)
        def _():
            sums = [part[1, h] + inbox[h] for h in heads]
            for h, both in zip(heads, sums):
                comb[h] = both

    def group_of(i):
        return lax.rem(x + 1 + i, NX)

    def heads_of(i):
        return [group_of(i) * NY + lax.rem(y + 1 + j, NY) for j in range(NY)]

    swaps = []

    def finish(i):
        swaps[i].wait_recv()

        @pl.when(core == 0)
        def _():
            here = pl.ds(group_of(i) * NY, NY)
            wait_bytes(mt_in.at[here], mt_sr.at[i])

        heads = heads_of(i)
        combine(heads)
        for j, h in enumerate(heads):
            if i == NX - 1 and j == NY - 1:
                fin[chip] = comb[h]
            else:
                remote(comb.at[h], fin.at[chip], e2_s, e2_r, h * NC + core).start()

        @pl.when(core == 0)
        def _():
            for j, h in enumerate(heads):
                if i == NX - 1 and j == NY - 1:
                    mt_f[chip] = mt_c[h]
                else:
                    remote(mt_c.at[h], mt_f.at[chip], e2t_s, e2t_r, h * NC).start()

    for i in range(NX):
        local_group(heads_of(i))
        block = pl.ds(group_of(i) * NY, NY)

        @pl.when(core == 1)
        def _():
            remote(mt_s.at[block], mt_in.at[block], mt_ss.at[i], mt_sr.at[i], partner).start()

        swap = remote(
            part.at[1 - core, block], inbox.at[block], sw_s.at[i], sw_r.at[i], partner
        )
        swap.start()
        swaps.append(swap)
    for i in range(NX):
        finish(i)

    ql_own = ql[chip]
    kl_own = kl[chip]
    scores = nt(ql_own, kl_own) * SCALE
    e = jnp.exp(scores - jnp.max(scores, axis=1, keepdims=True))
    a = e / jnp.sum(e, axis=1, keepdims=True)
    divisor = jnp.max(jnp.sum(a, axis=0, keepdims=True), axis=1, keepdims=True) * jnp.max(
        jnp.sum(a, axis=1, keepdims=True), axis=0, keepdims=True
    )
    a_t = a.T
    z = a_t / divisor
    unit = jnp.where(iota((M, M), 0) == iota((M, M), 1), 1.0, 0.0)
    sweeps = []
    for _ in range(ITERS):
        p = nn(a, z, HIGHEST)
        q1 = 7.0 * unit - p
        q2 = 15.0 * unit - nn(p, q1, HIGHEST)
        q3 = 13.0 * unit - nn(p, q2, HIGHEST)
        sweeps.append((z, p, q1, q2, q3))
        z = 0.25 * nn(z, q3, HIGHEST)
    left = jnp.where(core == 0, z, z.T)

    @pl.when(core == 1)
    def _():
        for k, (before, p, q1, q2, q3) in enumerate(sweeps):
            l0 = before.T
            l1 = nn(p, l0, HIGHEST)
            l2 = nn(p, l1, HIGHEST)
            s0, s1, s2 = [nn(a_t, l, HIGHEST) for l in (l0, l1, l2)]
            lefts[k] = jnp.concatenate([s0, s1, s2, l0, l1, l2], axis=0)
            steps[k] = 0.25 * jnp.concatenate([q3, -q2, q1, -unit], axis=0)
            sides[k] = 0.25 * jnp.concatenate(
                [7.0 * l1 - 15.0 * l0 - l2, 7.0 * l0 - l1, -l0], axis=0
            )

    wait_bytes(fin.at[0 : CHIPS - 1], e2_r)

    @pl.when(core == 0)
    def _():
        wait_bytes(mt_f.at[0 : CHIPS - 1], e2t_r)
        rows = jnp.concatenate([mt_f[s] for s in range(CHIPS)], axis=0)
        top = jnp.max(rows, axis=0, keepdims=True)
        factor = jnp.exp(rows - top)
        total = jnp.sum(factor * pltpu.roll(rows, M, 1), axis=0, keepdims=True)
        inverse = jnp.where(low, 1.0 / jnp.where(low, total, 1.0), 0.0)
        weight = nt(eye_low, factor * inverse, HIGHEST)
        summed = fin[0] * weight[:, 0:1]
        for s in range(1, CHIPS):
            summed = summed + fin[s] * weight[:, s : s + 1]
        sum_s[...] = summed
        stat[...] = jnp.where(low, top, pltpu.roll(inverse, M, 1))

    @pl.when(core == 1)
    def _():
        summed = fin[0]
        for s in range(1, CHIPS):
            summed = summed + fin[s]
        sum_s[...] = summed

    summed = sum_s[...]
    made = nn(left, summed, HIGHEST).astype(BF)
    res[...] = made
    ab[core, chip] = made
    spread(res, ab, e3_s, e3_r)

    def send_stat():
        sb[me] = stat[...]
        for offset in OFFSETS:
            remote(stat, sb.at[me], e3t_s, e3t_r.at[offset[0]], peer(offset)).start()

    @pl.when(core == 0)
    def _():
        cmat_out[...] = summed
        remote(cmat_out, cmat_in, cm_s, cm_r, partner).start()
        send_stat()
        wait_bytes(cmat_out, cm_s)

    @pl.when(core == 1)
    def _():
        wait_bytes(cmat_in, cm_r)
        c = cmat_in[...]
        dots = jnp.sum(made.astype(F32) * c, axis=1, keepdims=True)
        stat[...] = jnp.sum(jnp.where(diag_low, dots, 0.0), axis=0, keepdims=True)
        send_stat()
        grad = nt(summed, c, HIGHEST)
        a_grad = jnp.zeros((M, M), F32)
        for k in range(ITERS - 1, -1, -1):
            turned = nn(lefts[k], grad, HIGHEST)
            parts = [turned[i * M : (i + 1) * M] for i in range(6)]
            a_grad = a_grad + nn(jnp.concatenate(parts[3:], axis=1), sides[k], HIGHEST)
            grad = nn(jnp.concatenate([grad] + parts[:3], axis=1), steps[k], HIGHEST)
        a_grad = a_grad + grad.T / divisor
        a_score = a * (a_grad - jnp.sum(a * a_grad, axis=1, keepdims=True))
        asc_s[0] = nn(a_score, kl_own.astype(F32), HIGHEST) * SCALE
        asc_s[1] = nn(a_score.T, ql_own.astype(F32), HIGHEST) * SCALE

    shared, trades = {}, []

    def gradients(dx):
        row = lax.rem(x + NX - dx, NX) * NY
        slots = pl.ds(row * NC, NY * NC - (1 if dx == 0 else 0))
        wait_bytes(sb.at[slots], e3t_r.at[dx])
        shared[dx].wait_recv()
        heads = [row + j for j in range(NY)]
        alphas = []
        for h in heads:
            both = sb[NC * h]
            shift = jnp.exp(jnp.where(low, mt_s[h] - both, 0.0))
            alphas.append(jnp.where(low, shift * pltpu.roll(both, M, 1), 0.0))
        dots = [sb[NC * h + 1] for h in heads]
        cols = nt(eye_low, jnp.concatenate(alphas + dots, axis=0), HIGHEST)
        fgs = [nt(ab[0, h], g_v[:, head_cols(h)]) for h in heads]
        bgs = [nt(ab[1, h], v_v[:, head_cols(h)]) for h in heads]
        outs = []
        for j, (h, fg, bg) in enumerate(zip(heads, fgs, bgs)):
            fp = f_s[h]
            fs = (fp * (fg - jnp.sum(fp * fg, axis=0, keepdims=True))).astype(BF)
            bp = w_s[h] * cols[:, j : j + 1]
            bs = (bp * (bg - cols[:, NY + j : NY + j + 1])).astype(BF)
            kp = nn(fs, q_v[:, head_cols(h)]) * SCALE
            qp = nn(bs, k_v[:, head_cols(h)]) * SCALE
            outs.append((fs, bs, bp.astype(BF), qp, kp))
        for h, (fs, bs, bl, qp, kp) in zip(heads, outs):
            fs_s[h] = fs
            bs_s[h] = bs
            bl_s[h] = bl
            gpart[0, h] = qp
            gpart[1, h] = kp
        if dx == 0:

            @pl.when(core == 1)
            def _():
                for which in range(2):
                    gpart[which, chip] = gpart[which, chip] + asc_s[which]

        block = pl.ds(row, NY)
        trade = remote(
            gpart.at[1 - core, block], ginb.at[block], gs_s.at[dx], gs_r.at[dx], partner
        )
        trade.start()
        trades.append((trade, heads))

    for dx in (0, 1, 3, 2):
        shared[dx] = relay_row(ab, e3_s, e3_r, dx)
    for dx in (0, 1, 3, 2):
        gradients(dx)
    for trade, heads in trades:
        trade.wait_recv()
        for h in heads:
            s32[pl.ds(h, M, stride=H), :] = gpart[core, h] + ginb[h]
    for d in range(CHIPS):
        for c in range(NC):
            at = (d * NC + c) * 32
            s16[d, c] = s32[at : at + 32, :].astype(BF)
    r4[core * CHIPS + chip] = s16[chip, core]
    for offset in OFFSETS:
        target = peer(offset)
        remote(
            s16.at[target // NC, lax.rem(target, NC)], r4.at[core * CHIPS + chip],
            e4_s, e4_r, target,
        ).start()

    for h in range(H):
        at = slice(h * DH, (h + 1) * DH)
        att_v[:, at] = tn(f_s[h].astype(BF), ab[0, h]).astype(BF)
        vg_v[:, at] = tn(bl_s[h], ab[1, h]).astype(BF)
    for h in range(H):
        at = slice(h * DH, (h + 1) * DH)
        qg32[:, at] = tn(fs_s[h], kl[h]) * SCALE
        kg32[:, at] = tn(bs_s[h], ql[h]) * SCALE

    wait_bytes(r4.at[0 : GROUP - 1], e4_r)
    for c in range(NC):
        total = r4[c * CHIPS].astype(F32)
        for d in range(1, CHIPS):
            total = total + r4[c * CHIPS + d].astype(F32)
        land[c * 32 : (c + 1) * 32, :] = total * (1.0 / SEG)

    settle(rb, relays, e1_s)
    for swap in swaps:
        swap.wait_send()
    wait_bytes(fin.at[0 : CHIPS - 1], e2_s)

    @pl.when(core == 0)
    def _():
        wait_bytes(mt_f.at[0 : CHIPS - 1], e2t_s)

    @pl.when(core == 1)
    def _():
        for i in range(NX):
            wait_bytes(mt_s.at[pl.ds(0, NY)], mt_ss.at[i])

    settle(ab, list(shared.values()), e3_s)
    for trade, _ in trades:
        trade.wait_send()
    wait_bytes(sb.at[0 : GROUP - 1], e3t_s)
    wait_bytes(r4.at[0 : GROUP - 1], e4_s)


def finish_kernel(att, vg, qg32, kg32, land, att_out, qg_out, kg_out, vg_out, qg, kg, sem):
    copies = []

    def store(src, dst):
        copy = pltpu.make_async_copy(src, dst, sem.at[len(copies)])
        copy.start()
        copies.append(copy)

    store(att, att_out)
    store(vg, vg_out)
    for own, out, made, first in ((qg32, qg_out, qg, 0), (kg32, kg_out, kg, 2 * H)):
        for h in range(H):
            at = slice(h * DH, (h + 1) * DH)
            for seg in range(2):
                here = slice(seg * SEG, (seg + 1) * SEG)
                row = first + seg * H + h
                made[here, at] = (own[here, at] + land[row : row + 1, :]).astype(BF)
        store(made, out)
    for copy in copies:
        copy.wait()


def per_device(queries, keys, values, out_grad):
    shape = (ROWS, WIDTH)
    dma = pltpu.SemaphoreType.DMA
    rows = pltpu.VMEM(shape, BF)
    scratch = (
        [rows] * 4
        + [pltpu.VMEM((64, DH), F32), pltpu.VMEM((64, DH), BF)]
        + [pltpu.VMEM((NC, CHIPS, 64, DH), BF), pltpu.VMEM((2, M * H, DH), F32)]
        + [pltpu.VMEM((H, M, DH), BF)] * 2
        + [pltpu.VMEM((H, M, ROWS), F32)] * 2
        + [pltpu.VMEM((2, H, M, DH), F32)]
        + [pltpu.VMEM((H, M, DH), F32)] * 3
        + [pltpu.VMEM((H, 1, DH), F32)] * 4
        + [pltpu.VMEM((M, DH), F32)]
        + [pltpu.VMEM((ITERS, n * M, M), F32) for n in (6, 4, 3)]
        + [pltpu.VMEM((M, DH), BF), pltpu.VMEM((1, DH), F32)]
        + [pltpu.VMEM((M, DH), F32)] * 2
        + [pltpu.VMEM((NC, CHIPS, M, DH), BF), pltpu.VMEM((GROUP, 1, DH), F32)]
        + [pltpu.VMEM((2, H, M, DH), F32), pltpu.VMEM((H, M, DH), F32)]
        + [pltpu.VMEM((M * H, DH), F32)]
        + [pltpu.VMEM((CHIPS, NC, 32, DH), BF), pltpu.VMEM((GROUP, 32, DH), BF)]
        + [pltpu.VMEM((H, M, ROWS), BF)] * 3
        + [pltpu.VMEM((2, M, DH), F32)]
        + [dma((4,)), dma((NX + 1,)), dma((2 * NX,))]
        + [dma((NX,))] * 4
        + [dma] * 4
        + [dma] * 2
        + [dma((NX + 1,)), dma((2 * NX,)), dma, dma((NX,))]
        + [dma((NX,))] * 2
        + [dma] * 2
    )
    made = pl.pallas_call(
        kernel,
        out_shape=[pltpu.VMEM(shape, BF)] * 2
        + [pltpu.VMEM(shape, F32)] * 2
        + [pltpu.VMEM((64, DH), F32)],
        in_specs=[pl.BlockSpec(memory_space=pl.ANY)] * 4,
        out_specs=[pl.BlockSpec(memory_space=pltpu.VMEM)] * 5,
        scratch_shapes=scratch,
        compiler_params=pltpu.CompilerParams(
            collective_id=0, has_side_effects=True, vmem_limit_bytes=30 << 20
        ),
    )(*[pltpu.with_memory_space_constraint(a, pltpu.HBM) for a in (queries, keys, values, out_grad)])
    return pl.pallas_call(
        finish_kernel,
        out_shape=[jax.ShapeDtypeStruct(shape, BF)] * 4,
        in_specs=[pl.BlockSpec(memory_space=pltpu.VMEM)] * 5,
        out_specs=[pl.BlockSpec(memory_space=pl.ANY)] * 4,
        scratch_shapes=[rows] * 2 + [dma((4,))],
        compiler_params=pltpu.CompilerParams(vmem_limit_bytes=8 << 20),
    )(*made)


def solution(mesh):
    placed = P(("doc", "ctx"), None)
    return jax.shard_map(
        per_device,
        mesh=mesh,
        in_specs=(placed,) * 4,
        out_specs=(placed,) * 4,
        check_vma=False,
    )
```

```python
import jax
import jax.numpy as jnp
from jax import lax
from jax.experimental import pallas as pl
from jax.experimental.pallas import tpu as pltpu
from jax.sharding import PartitionSpec as P

H = 16
DH = 128
M = 64
ITERS = 6
SCALE = DH ** (-0.5)
MESH = pl.DeviceIdType.MESH
HIGHEST = lax.Precision.HIGHEST
BF = jnp.bfloat16
F32 = jnp.float32
NX, NY, NC = 4, 4, 2
CHIPS = NX * NY
GROUP = CHIPS * NC
ROWS = 128
SEG = 64
WIDTH = H * DH

STEPS = [
    (2, 2), (2, 1), (1, 2), (2, 3), (3, 2), (2, 0), (0, 2), (1, 1),
    (3, 3), (1, 3), (3, 1), (1, 0), (0, 1), (3, 0), (0, 3), (0, 0),
]
OTHERS = STEPS[:-1]
OFFSETS = [(dx, dy, dc) for dx, dy in OTHERS for dc in range(NC)] + [(0, 0, 1)]


def nn(a, b, precision=None):
    return lax.dot_general(
        a, b, (((1,), (0,)), ((), ())), precision=precision, preferred_element_type=F32
    )


def nt(a, b, precision=None):
    return lax.dot_general(
        a, b, (((1,), (1,)), ((), ())), precision=precision, preferred_element_type=F32
    )


def tn(a, b, precision=None):
    return lax.dot_general(
        a, b, (((0,), (0,)), ((), ())), precision=precision, preferred_element_type=F32
    )


def iota(shape, dim):
    return lax.broadcasted_iota(jnp.int32, shape, dim)


def wait_bytes(ref, sem):
    pltpu.make_async_copy(ref, ref, sem).wait()


def head_cols(h):
    return pl.ds(pl.multiple_of(h * DH, DH), DH)


def kernel(
    q_hbm, k_hbm, v_hbm, g_hbm,
    att_v, vg_v, qg32, kg32, land,
    q_v, k_v, a_v, b_v,
    msg32, msg16, rb, lf, lm, lm_in,
    w_s, part, fin, mt_s, mt_f, sum_s,
    lefts, steps, sides,
    res, stat, cmat_in, cmat_out, ab, sb,
    s32, s16, r4, bs_s, bl_s, asc_out, asc_in, asc_s, x1_s, x2_s,
    in_sem, pre_s, pre_r, e1_s, e1_r, lm_ss, lm_sr, e2_s, e2_r, e2t_s, e2t_r,
    cm_s, cm_r, e3_s, e3_r, e3t_s, e3t_r, as_s, as_r, e4_s, e4_r, x_s, x_r,
):
    me = lax.axis_index("ctx")
    core = lax.rem(me, NC)
    chip = me // NC
    y = lax.rem(chip, NY)
    x = chip // NY
    partner = chip * NC + (1 - core)

    def chip_at(dx, dy):
        return lax.rem(x + dx, NX) * NY + lax.rem(y + dy, NY)

    def peer(offset):
        dx, dy, dc = offset
        return chip_at(dx, dy) * NC + lax.rem(core + dc, NC)

    def remote(src, dst, send, recv, target):
        return pltpu.make_async_remote_copy(
            src_ref=src, dst_ref=dst, send_sem=send, recv_sem=recv,
            device_id={"ctx": target}, device_id_type=MESH,
        )

    barrier = pltpu.get_barrier_semaphore()
    for offset in OFFSETS:
        pl.semaphore_signal(
            barrier, inc=1, device_id={"ctx": peer(offset)}, device_id_type=MESH
        )
    load_q = pltpu.make_async_copy(q_hbm, q_v, in_sem.at[0])
    load_k = pltpu.make_async_copy(k_hbm, k_v, in_sem.at[1])
    load_q.start()
    load_k.start()
    mine = pl.ds(pl.multiple_of(core * ROWS, ROWS), ROWS)

    @pl.when(core == 0)
    def _():
        pltpu.make_async_copy(k_hbm, a_v.at[0:ROWS], in_sem.at[2]).start()
        pltpu.make_async_copy(v_hbm, b_v.at[0:ROWS], in_sem.at[3]).start()

    @pl.when(core == 1)
    def _():
        pltpu.make_async_copy(q_hbm, a_v.at[ROWS : 2 * ROWS], in_sem.at[2]).start()
        pltpu.make_async_copy(g_hbm, b_v.at[ROWS : 2 * ROWS], in_sem.at[3]).start()

    pick = jnp.where(iota((8, ROWS), 0) == iota((8, ROWS), 1) // SEG, 1.0, 0.0).astype(BF)
    for which, load, ref in ((0, load_q, q_v), (1, load_k, k_v)):
        load.wait()
        sums = nn(pick, ref[...]) * (1.0 / SEG)
        for seg in range(2):
            for h in range(H):
                row = seg * H + h
                msg32[which, row : row + 1, :] = sums[seg : seg + 1, h * DH : (h + 1) * DH]
    msg16[...] = msg32[...].astype(BF)
    rb[me] = msg16[core]
    pl.semaphore_wait(barrier, GROUP - 1)
    for offset in OFFSETS:
        target = peer(offset)
        remote(msg16.at[lax.rem(target, NC)], rb.at[me], e1_s, e1_r, target).start()

    @pl.when(core == 0)
    def _():
        remote(q_hbm, a_v.at[0:ROWS], pre_s.at[0], pre_r.at[0], partner).start()
        remote(g_hbm, b_v.at[0:ROWS], pre_s.at[1], pre_r.at[1], partner).start()

    @pl.when(core == 1)
    def _():
        remote(k_hbm, a_v.at[ROWS : 2 * ROWS], pre_s.at[0], pre_r.at[0], partner).start()
        remote(v_hbm, b_v.at[ROWS : 2 * ROWS], pre_s.at[1], pre_r.at[1], partner).start()

    wait_bytes(a_v.at[mine], in_sem.at[2])
    wait_bytes(b_v.at[mine], in_sem.at[3])
    for slot, ref in ((0, a_v), (1, b_v)):
        wait_bytes(ref.at[0:ROWS], pre_r.at[slot])
    wait_bytes(rb.at[0 : GROUP - 1], e1_r)
    for d in range(GROUP):
        lf[d * 32 : (d + 1) * 32, :] = rb[d].astype(F32)
    for h in range(H):
        lm[h] = lf[pl.ds(h, M, stride=H), :].astype(BF)
    hand = remote(lm.at[chip], lm_in, lm_ss, lm_sr, partner)
    hand.start()

    row_at = iota((M, DH), 0)
    lane_at = iota((M, DH), 1)
    diag_low = lane_at == row_at
    diag_high = lane_at == row_at + M
    low = iota((1, DH), 1) < M
    eye_low = jnp.where(diag_low, 1.0, 0.0)

    def value_group(heads):
        scores = [nt(lm[h], a_v[:, head_cols(h)]) * SCALE for h in heads]
        outs = []
        for h, s in zip(heads, scores):
            m = jnp.max(s, axis=1, keepdims=True)
            w = jnp.exp(s - m)
            t = jnp.sum(w, axis=1, keepdims=True)
            hi = w.astype(BF)
            lo = (w - hi.astype(F32)).astype(BF)
            vals = b_v[:, head_cols(h)]
            sums = nn(hi, vals) + nn(lo, vals)
            row = jnp.sum(
                jnp.where(diag_low, m, 0.0) + jnp.where(diag_high, t, 0.0), axis=0, keepdims=True
            )
            outs.append((w, sums, row))
        for h, (w, sums, row) in zip(heads, outs):
            w_s[h] = w
            part[h] = sums
            mt_s[h] = row

    def gradient_group(heads):
        scores = [nt(lm[h], a_v[:, head_cols(h)]) * SCALE for h in heads]
        outs = []
        for h, s in zip(heads, scores):
            e = jnp.exp(s - jnp.max(s, axis=0, keepdims=True))
            prob = e / jnp.sum(e, axis=0, keepdims=True)
            outs.append((prob, nn(prob.astype(BF), b_v[:, head_cols(h)])))
        for h, (prob, sums) in zip(heads, outs):
            w_s[h] = prob
            part[h] = sums

    for i in range(NX):
        group = STEPS[i * NY : (i + 1) * NY]
        heads = [chip_at(*step) for step in group]

        @pl.when(core == 0)
        def _():
            value_group(heads)
            for step, h in zip(group, heads):
                if step == (0, 0):
                    mt_f[chip] = mt_s[h]
                else:
                    remote(mt_s.at[h], mt_f.at[chip], e2t_s, e2t_r, h * NC).start()

        @pl.when(core == 1)
        def _():
            gradient_group(heads)

        for step, h in zip(group, heads):
            if step == (0, 0):
                fin[chip] = part[h]
            else:
                remote(part.at[h], fin.at[chip], e2_s, e2_r, h * NC + core).start()

    hand.wait_recv()
    own = lm[chip].astype(F32)
    other = lm_in[...].astype(F32)
    ql_own = jnp.where(core == 0, own, other)
    kl_own = jnp.where(core == 0, other, own)
    scores = nt(ql_own.astype(BF), kl_own.astype(BF)) * SCALE
    e = jnp.exp(scores - jnp.max(scores, axis=1, keepdims=True))
    a = e / jnp.sum(e, axis=1, keepdims=True)
    divisor = jnp.max(jnp.sum(a, axis=0, keepdims=True), axis=1, keepdims=True) * jnp.max(
        jnp.sum(a, axis=1, keepdims=True), axis=0, keepdims=True
    )
    a_t = a.T
    z = a_t / divisor
    unit = jnp.where(iota((M, M), 0) == iota((M, M), 1), 1.0, 0.0)
    sweeps = []
    for _ in range(ITERS):
        p = nn(a, z, HIGHEST)
        q1 = 7.0 * unit - p
        q2 = 15.0 * unit - nn(p, q1, HIGHEST)
        q3 = 13.0 * unit - nn(p, q2, HIGHEST)
        sweeps.append((z, p, q1, q2, q3))
        z = 0.25 * nn(z, q3, HIGHEST)
    left = jnp.where(core == 0, z, z.T)

    @pl.when(core == 1)
    def _():
        for k, (before, p, q1, q2, q3) in enumerate(sweeps):
            l0 = before.T
            l1 = nn(p, l0, HIGHEST)
            l2 = nn(p, l1, HIGHEST)
            s0, s1, s2 = [nn(a_t, l, HIGHEST) for l in (l0, l1, l2)]
            lefts[k] = jnp.concatenate([s0, s1, s2, l0, l1, l2], axis=0)
            steps[k] = 0.25 * jnp.concatenate([q3, -q2, q1, -unit], axis=0)
            sides[k] = 0.25 * jnp.concatenate(
                [7.0 * l1 - 15.0 * l0 - l2, 7.0 * l0 - l1, -l0], axis=0
            )

    wait_bytes(fin.at[0 : CHIPS - 1], e2_r)

    @pl.when(core == 0)
    def _():
        wait_bytes(mt_f.at[0 : CHIPS - 1], e2t_r)
        rows = jnp.concatenate([mt_f[s] for s in range(CHIPS)], axis=0)
        top = jnp.max(rows, axis=0, keepdims=True)
        factor = jnp.exp(rows - top)
        total = jnp.sum(factor * pltpu.roll(rows, M, 1), axis=0, keepdims=True)
        inverse = jnp.where(low, 1.0 / jnp.where(low, total, 1.0), 0.0)
        weight = nt(eye_low, factor * inverse, HIGHEST)
        summed = fin[0] * weight[:, 0:1]
        for s in range(1, CHIPS):
            summed = summed + fin[s] * weight[:, s : s + 1]
        sum_s[...] = summed
        stat[...] = jnp.where(low, top, pltpu.roll(inverse, M, 1))

    @pl.when(core == 1)
    def _():
        summed = fin[0]
        for s in range(1, CHIPS):
            summed = summed + fin[s]
        sum_s[...] = summed

    summed = sum_s[...]
    made = nn(left, summed, HIGHEST).astype(BF)
    res[...] = made
    for dx, dy in STEPS:
        remote(res, ab.at[chip], e3_s, e3_r.at[dx], peer((dx, dy, 1))).start()

    @pl.when(core == 0)
    def _():
        cmat_out[...] = summed
        remote(cmat_out, cmat_in, cm_s, cm_r, partner).start()
        sb[chip] = stat[...]
        for dx, dy in OTHERS:
            remote(stat, sb.at[chip], e3t_s, e3t_r.at[dx], peer((dx, dy, 0))).start()
        wait_bytes(cmat_out, cm_s)

    @pl.when(core == 1)
    def _():
        wait_bytes(cmat_in, cm_r)
        c = cmat_in[...]
        dots = jnp.sum(made.astype(F32) * c, axis=1, keepdims=True)
        stat[...] = jnp.sum(jnp.where(diag_low, dots, 0.0), axis=0, keepdims=True)
        for dx, dy in STEPS:
            remote(stat, sb.at[CHIPS + chip], e3t_s, e3t_r.at[dx], peer((dx, dy, 1))).start()
        grad = nt(summed, c, HIGHEST)
        a_grad = jnp.zeros((M, M), F32)
        for k in range(ITERS - 1, -1, -1):
            turned = nn(lefts[k], grad, HIGHEST)
            parts = [turned[i * M : (i + 1) * M] for i in range(6)]
            a_grad = a_grad + nn(jnp.concatenate(parts[3:], axis=1), sides[k], HIGHEST)
            grad = nn(jnp.concatenate([grad] + parts[:3], axis=1), steps[k], HIGHEST)
        a_grad = a_grad + grad.T / divisor
        a_score = a * (a_grad - jnp.sum(a * a_grad, axis=1, keepdims=True))
        asc_out[...] = nn(a_score, kl_own, HIGHEST) * SCALE
        remote(asc_out, asc_in, as_s, as_r, partner).start()
        asc_s[...] = nn(a_score.T, ql_own, HIGHEST) * SCALE

    for dx in (0, 1, 3, 2):
        row = lax.rem(x + NX - dx, NX) * NY
        heads = [row + j for j in range(NY)]
        wait_bytes(ab.at[0:NY], e3_r.at[dx])

        @pl.when(core == 0)
        def _():
            wait_bytes(sb.at[0 : (2 * NY - 1 if dx == 0 else 2 * NY)], e3t_r.at[dx])
            alphas = []
            for h in heads:
                both = sb[h]
                shift = jnp.exp(jnp.where(low, mt_s[h] - both, 0.0))
                alphas.append(jnp.where(low, shift * pltpu.roll(both, M, 1), 0.0))
            dots = [sb[CHIPS + h] for h in heads]
            cols = nt(eye_low, jnp.concatenate(alphas + dots, axis=0), HIGHEST)
            grads = [nt(ab[h], b_v[:, head_cols(h)]) for h in heads]
            outs = []
            for j, (h, bg) in enumerate(zip(heads, grads)):
                prob = w_s[h] * cols[:, j : j + 1]
                score = (prob * (bg - cols[:, NY + j : NY + j + 1])).astype(BF)
                outs.append((prob.astype(BF), score, nn(score, a_v[:, head_cols(h)]) * SCALE))
            for h, (prob, score, sums) in zip(heads, outs):
                bl_s[h] = prob
                bs_s[h] = score
                s32[pl.ds(h, M, stride=H), :] = sums

        @pl.when(core == 1)
        def _():
            grads = [nt(ab[h], b_v[:, head_cols(h)]) for h in heads]
            outs = []
            for h, fg in zip(heads, grads):
                prob = w_s[h]
                score = (prob * (fg - jnp.sum(prob * fg, axis=0, keepdims=True))).astype(BF)
                outs.append((prob.astype(BF), score, nn(score, a_v[:, head_cols(h)]) * SCALE))
            for h, (prob, score, sums) in zip(heads, outs):
                bl_s[h] = prob
                bs_s[h] = score
                s32[pl.ds(h, M, stride=H), :] = sums

    @pl.when(core == 0)
    def _():
        wait_bytes(asc_in, as_r)
        asc_s[...] = asc_in[...]

    at_own = pl.ds(chip, M, stride=H)
    s32[at_own, :] = s32[at_own, :] + asc_s[...]
    for d in range(CHIPS):
        for c in range(NC):
            at = (d * NC + c) * 32
            s16[d, c] = s32[at : at + 32, :].astype(BF)
    r4[core * CHIPS + chip] = s16[chip, core]
    for offset in OFFSETS:
        target = peer(offset)
        remote(
            s16.at[target // NC, lax.rem(target, NC)], r4.at[core * CHIPS + chip],
            e4_s, e4_r, target,
        ).start()

    for first in range(0, H, 4):
        for h in range(first, first + 4):
            at = slice(h * DH, (h + 1) * DH)
            part2 = tn(bs_s[h], lm[h]) * SCALE
            part1 = tn(bl_s[h], ab[h]).astype(BF)
            for c in range(NC):
                x2_s[c, :, at] = part2[c * ROWS : (c + 1) * ROWS]
                x1_s[c, :, at] = part1[c * ROWS : (c + 1) * ROWS]
        cols = pl.ds(first * DH, 4 * DH)

        def move(kept1, kept2, given1, given2, c):
            for slot, (src, kept, given) in enumerate(
                ((x1_s, kept1, given1), (x2_s, kept2, given2))
            ):
                remote(
                    src.at[1 - c, :, cols], given.at[:, cols], x_s.at[slot], x_r.at[slot], partner
                ).start()
                pltpu.make_async_copy(
                    src.at[c, :, cols], kept.at[:, cols], x_s.at[2 + slot]
                ).start()

        @pl.when(core == 0)
        def _():
            move(vg_v, kg32, vg_v, kg32, 0)

        @pl.when(core == 1)
        def _():
            move(att_v, qg32, att_v, qg32, 1)

    wait_bytes(r4.at[0 : GROUP - 1], e4_r)
    for c in range(NC):
        total = r4[c * CHIPS].astype(F32)
        for d in range(1, CHIPS):
            total = total + r4[c * CHIPS + d].astype(F32)
        land[c * 32 : (c + 1) * 32, :] = total * (1.0 / SEG)

    for slot, ref in ((0, x1_s), (1, x2_s)):
        wait_bytes(ref.at[0], x_r.at[slot])
        wait_bytes(ref.at[0], x_s.at[slot])
        wait_bytes(ref.at[0], x_s.at[2 + slot])
    for slot, ref in ((0, a_v), (1, b_v)):
        wait_bytes(ref.at[0:ROWS], pre_s.at[slot])
    wait_bytes(rb.at[0 : GROUP - 1], e1_s)
    hand.wait_send()
    wait_bytes(fin.at[0 : CHIPS - 1], e2_s)
    wait_bytes(ab.at[0:CHIPS], e3_s)

    @pl.when(core == 0)
    def _():
        wait_bytes(mt_f.at[0 : CHIPS - 1], e2t_s)
        wait_bytes(sb.at[0 : CHIPS - 1], e3t_s)

    @pl.when(core == 1)
    def _():
        wait_bytes(sb.at[0:CHIPS], e3t_s)
        wait_bytes(asc_out, as_s)

    wait_bytes(r4.at[0 : GROUP - 1], e4_s)


def finish_kernel(att, vg, qg32, kg32, land, att_out, qg_out, kg_out, vg_out, qg, kg, sem):
    copies = []

    def store(src, dst):
        copy = pltpu.make_async_copy(src, dst, sem.at[len(copies)])
        copy.start()
        copies.append(copy)

    store(att, att_out)
    store(vg, vg_out)
    for own, out, made, first in ((qg32, qg_out, qg, 0), (kg32, kg_out, kg, 2 * H)):
        for h in range(H):
            at = slice(h * DH, (h + 1) * DH)
            for seg in range(2):
                here = slice(seg * SEG, (seg + 1) * SEG)
                row = first + seg * H + h
                made[here, at] = (own[here, at] + land[row : row + 1, :]).astype(BF)
        store(made, out)
    for copy in copies:
        copy.wait()


def per_device(queries, keys, values, out_grad):
    shape = (ROWS, WIDTH)
    dma = pltpu.SemaphoreType.DMA
    rows = pltpu.VMEM(shape, BF)
    square = pltpu.VMEM((M, DH), F32)
    scratch = (
        [rows] * 2
        + [pltpu.VMEM((NC * ROWS, WIDTH), BF)] * 2
        + [pltpu.VMEM((2, 32, DH), F32), pltpu.VMEM((2, 32, DH), BF)]
        + [pltpu.VMEM((GROUP, 32, DH), BF), pltpu.VMEM((M * H, DH), F32)]
        + [pltpu.VMEM((H, M, DH), BF), pltpu.VMEM((M, DH), BF)]
        + [pltpu.VMEM((H, M, NC * ROWS), F32)]
        + [pltpu.VMEM((H, M, DH), F32)] * 2
        + [pltpu.VMEM((H, 1, DH), F32)] * 2
        + [square]
        + [pltpu.VMEM((ITERS, n * M, M), F32) for n in (6, 4, 3)]
        + [pltpu.VMEM((M, DH), BF), pltpu.VMEM((1, DH), F32)]
        + [square] * 2
        + [pltpu.VMEM((CHIPS, M, DH), BF), pltpu.VMEM((GROUP, 1, DH), F32)]
        + [pltpu.VMEM((M * H, DH), F32)]
        + [pltpu.VMEM((CHIPS, NC, 32, DH), BF), pltpu.VMEM((GROUP, 32, DH), BF)]
        + [pltpu.VMEM((H, M, NC * ROWS), BF)] * 2
        + [square] * 3
        + [pltpu.VMEM((NC,) + shape, BF), pltpu.VMEM((NC,) + shape, F32)]
        + [dma((4,)), dma((2,)), dma((2,))]
        + [dma] * 8
        + [dma] * 2
        + [dma, dma((NX,)), dma, dma((NX,))]
        + [dma] * 4
        + [dma((4,)), dma((2,))]
    )
    made = pl.pallas_call(
        kernel,
        out_shape=[pltpu.VMEM(shape, BF)] * 2
        + [pltpu.VMEM(shape, F32)] * 2
        + [pltpu.VMEM((64, DH), F32)],
        in_specs=[pl.BlockSpec(memory_space=pl.ANY)] * 4,
        out_specs=[pl.BlockSpec(memory_space=pltpu.VMEM)] * 5,
        scratch_shapes=scratch,
        compiler_params=pltpu.CompilerParams(
            collective_id=0, has_side_effects=True, vmem_limit_bytes=30 << 20
        ),
    )(*[pltpu.with_memory_space_constraint(a, pltpu.HBM) for a in (queries, keys, values, out_grad)])
    return pl.pallas_call(
        finish_kernel,
        out_shape=[jax.ShapeDtypeStruct(shape, BF)] * 4,
        in_specs=[pl.BlockSpec(memory_space=pltpu.VMEM)] * 5,
        out_specs=[pl.BlockSpec(memory_space=pl.ANY)] * 4,
        scratch_shapes=[rows] * 2 + [dma((4,))],
        compiler_params=pltpu.CompilerParams(vmem_limit_bytes=8 << 20),
    )(*made)


def solution(mesh):
    placed = P(("doc", "ctx"), None)
    return jax.shard_map(
        per_device,
        mesh=mesh,
        in_specs=(placed,) * 4,
        out_specs=(placed,) * 4,
        check_vma=False,
    )
```

```python
import jax
import jax.numpy as jnp
from jax import lax
from jax.experimental import pallas as pl
from jax.experimental.pallas import tpu as pltpu
from jax.sharding import PartitionSpec as P

H = 16
DH = 128
M = 64
ITERS = 6
SCALE = DH ** (-0.5)
MESH = pl.DeviceIdType.MESH
HIGHEST = lax.Precision.HIGHEST
BF = jnp.bfloat16
F32 = jnp.float32
NX, NY, NC = 4, 4, 2
CHIPS = NX * NY
GROUP = CHIPS * NC
ROWS = 128
SEG = 64
WIDTH = H * DH

STEPS = [
    (2, 2), (2, 1), (1, 2), (2, 3), (3, 2), (2, 0), (0, 2), (1, 1),
    (3, 3), (1, 3), (3, 1), (1, 0), (0, 1), (3, 0), (0, 3), (0, 0),
]
OTHERS = STEPS[:-1]
OFFSETS = [(dx, dy, dc) for dx, dy in OTHERS for dc in range(NC)] + [(0, 0, 1)]


def nn(a, b, precision=None):
    return lax.dot_general(
        a, b, (((1,), (0,)), ((), ())), precision=precision, preferred_element_type=F32
    )


def nt(a, b, precision=None):
    return lax.dot_general(
        a, b, (((1,), (1,)), ((), ())), precision=precision, preferred_element_type=F32
    )


def tn(a, b, precision=None):
    return lax.dot_general(
        a, b, (((0,), (0,)), ((), ())), precision=precision, preferred_element_type=F32
    )


def halves(a):
    hi = a.astype(BF)
    return hi, (a - hi.astype(F32)).astype(BF)


def by_halves(blocks, right_hi, right_lo):
    hi, lo = halves(jnp.concatenate(blocks, axis=1))
    return nn(hi, right_hi) + (nn(lo, right_hi) + nn(hi, right_lo))


def iota(shape, dim):
    return lax.broadcasted_iota(jnp.int32, shape, dim)


def wait_bytes(ref, sem):
    pltpu.make_async_copy(ref, ref, sem).wait()


def head_cols(h):
    return pl.ds(pl.multiple_of(h * DH, DH), DH)


def kernel(
    q_hbm, k_hbm, v_hbm, g_hbm,
    att_v, vg_v, qg32, kg32, land,
    q_v, k_v, a_v, b_v,
    msg32, msg16, rb, lf, lm, lm_in,
    w_s, part, fin, mt_s, mt_f, sum_s,
    lefts, steps, sides,
    res, stat, cmat_in, cmat_out, ab, sb,
    s32, s16, r4, bs_s, bl_s, asc_out, asc_in, asc_s, x1_s, x2_s,
    in_sem, pre_s, pre_r, e1_s, e1_r, lm_ss, lm_sr, e2_s, e2_r, e2t_s, e2t_r,
    cm_s, cm_r, e3_s, e3_r, e3t_s, e3t_r, as_s, as_r, e4_s, e4_r, x_s, x_r,
):
    me = lax.axis_index("ctx")
    core = lax.rem(me, NC)
    chip = me // NC
    y = lax.rem(chip, NY)
    x = chip // NY
    partner = chip * NC + (1 - core)

    def chip_at(dx, dy):
        return lax.rem(x + dx, NX) * NY + lax.rem(y + dy, NY)

    def peer(offset):
        dx, dy, dc = offset
        return chip_at(dx, dy) * NC + lax.rem(core + dc, NC)

    def remote(src, dst, send, recv, target):
        return pltpu.make_async_remote_copy(
            src_ref=src, dst_ref=dst, send_sem=send, recv_sem=recv,
            device_id={"ctx": target}, device_id_type=MESH,
        )

    barrier = pltpu.get_barrier_semaphore()
    for offset in OFFSETS:
        pl.semaphore_signal(
            barrier, inc=1, device_id={"ctx": peer(offset)}, device_id_type=MESH
        )
    load_q = pltpu.make_async_copy(q_hbm, q_v, in_sem.at[0])
    load_k = pltpu.make_async_copy(k_hbm, k_v, in_sem.at[1])
    load_q.start()
    load_k.start()
    mine = pl.ds(pl.multiple_of(core * ROWS, ROWS), ROWS)

    @pl.when(core == 0)
    def _():
        pltpu.make_async_copy(k_hbm, a_v.at[0:ROWS], in_sem.at[2]).start()
        pltpu.make_async_copy(v_hbm, b_v.at[0:ROWS], in_sem.at[3]).start()

    @pl.when(core == 1)
    def _():
        pltpu.make_async_copy(q_hbm, a_v.at[ROWS : 2 * ROWS], in_sem.at[2]).start()
        pltpu.make_async_copy(g_hbm, b_v.at[ROWS : 2 * ROWS], in_sem.at[3]).start()

    pick = jnp.where(iota((8, ROWS), 0) == iota((8, ROWS), 1) // SEG, 1.0, 0.0).astype(BF)
    for which, load, ref in ((0, load_q, q_v), (1, load_k, k_v)):
        load.wait()
        sums = nn(pick, ref[...]) * (1.0 / SEG)
        for seg in range(2):
            for h in range(H):
                row = seg * H + h
                msg32[which, row : row + 1, :] = sums[seg : seg + 1, h * DH : (h + 1) * DH]
    msg16[...] = msg32[...].astype(BF)
    rb[me] = msg16[core]
    pl.semaphore_wait(barrier, GROUP - 1)
    for offset in OFFSETS:
        target = peer(offset)
        remote(msg16.at[lax.rem(target, NC)], rb.at[me], e1_s, e1_r, target).start()

    @pl.when(core == 0)
    def _():
        remote(q_hbm, a_v.at[0:ROWS], pre_s.at[0], pre_r.at[0], partner).start()
        remote(g_hbm, b_v.at[0:ROWS], pre_s.at[1], pre_r.at[1], partner).start()

    @pl.when(core == 1)
    def _():
        remote(k_hbm, a_v.at[ROWS : 2 * ROWS], pre_s.at[0], pre_r.at[0], partner).start()
        remote(v_hbm, b_v.at[ROWS : 2 * ROWS], pre_s.at[1], pre_r.at[1], partner).start()

    wait_bytes(a_v.at[mine], in_sem.at[2])
    wait_bytes(b_v.at[mine], in_sem.at[3])
    for slot, ref in ((0, a_v), (1, b_v)):
        wait_bytes(ref.at[0:ROWS], pre_r.at[slot])
    wait_bytes(rb.at[0 : GROUP - 1], e1_r)
    for d in range(GROUP):
        lf[d * 32 : (d + 1) * 32, :] = rb[d].astype(F32)
    for h in range(H):
        lm[h] = lf[pl.ds(h, M, stride=H), :].astype(BF)
    hand = remote(lm.at[chip], lm_in, lm_ss, lm_sr, partner)
    hand.start()

    row_at = iota((M, DH), 0)
    lane_at = iota((M, DH), 1)
    diag_low = lane_at == row_at
    diag_high = lane_at == row_at + M
    low = iota((1, DH), 1) < M
    eye_low = jnp.where(diag_low, 1.0, 0.0)

    def value_group(heads):
        scores = [nt(lm[h], a_v[:, head_cols(h)]) * SCALE for h in heads]
        outs = []
        for h, s in zip(heads, scores):
            m = jnp.max(s, axis=1, keepdims=True)
            w = jnp.exp(s - m)
            t = jnp.sum(w, axis=1, keepdims=True)
            hi = w.astype(BF)
            lo = (w - hi.astype(F32)).astype(BF)
            vals = b_v[:, head_cols(h)]
            sums = nn(hi, vals) + nn(lo, vals)
            row = jnp.sum(
                jnp.where(diag_low, m, 0.0) + jnp.where(diag_high, t, 0.0), axis=0, keepdims=True
            )
            outs.append((w, sums, row))
        for h, (w, sums, row) in zip(heads, outs):
            w_s[h] = w
            part[h] = sums
            mt_s[h] = row

    def gradient_group(heads):
        scores = [nt(lm[h], a_v[:, head_cols(h)]) * SCALE for h in heads]
        outs = []
        for h, s in zip(heads, scores):
            e = jnp.exp(s - jnp.max(s, axis=0, keepdims=True))
            prob = e / jnp.sum(e, axis=0, keepdims=True)
            outs.append((prob, nn(prob.astype(BF), b_v[:, head_cols(h)])))
        for h, (prob, sums) in zip(heads, outs):
            w_s[h] = prob
            part[h] = sums

    for i in range(NX):
        group = STEPS[i * NY : (i + 1) * NY]
        heads = [chip_at(*step) for step in group]

        @pl.when(core == 0)
        def _():
            value_group(heads)
            for step, h in zip(group, heads):
                if step == (0, 0):
                    mt_f[chip] = mt_s[h]
                else:
                    remote(mt_s.at[h], mt_f.at[chip], e2t_s, e2t_r, h * NC).start()

        @pl.when(core == 1)
        def _():
            gradient_group(heads)

        for step, h in zip(group, heads):
            if step == (0, 0):
                fin[chip] = part[h]
            else:
                remote(part.at[h], fin.at[chip], e2_s, e2_r, h * NC + core).start()

    hand.wait_recv()
    own = lm[chip].astype(F32)
    other = lm_in[...].astype(F32)
    ql_own = jnp.where(core == 0, own, other)
    kl_own = jnp.where(core == 0, other, own)
    scores = nt(ql_own.astype(BF), kl_own.astype(BF)) * SCALE
    e = jnp.exp(scores - jnp.max(scores, axis=1, keepdims=True))
    a = e / jnp.sum(e, axis=1, keepdims=True)
    divisor = jnp.max(jnp.sum(a, axis=0, keepdims=True), axis=1, keepdims=True) * jnp.max(
        jnp.sum(a, axis=1, keepdims=True), axis=0, keepdims=True
    )
    a_t = a.T
    z = a_t / divisor
    unit = jnp.where(iota((M, M), 0) == iota((M, M), 1), 1.0, 0.0)
    sweeps = []
    for _ in range(ITERS):
        p = nn(a, z, HIGHEST)
        q1 = 7.0 * unit - p
        q2 = 15.0 * unit - nn(p, q1, HIGHEST)
        q3 = 13.0 * unit - nn(p, q2, HIGHEST)
        sweeps.append((z, p, q1, q2, q3))
        z = 0.25 * nn(z, q3, HIGHEST)
    left = jnp.where(core == 0, z, z.T)

    @pl.when(core == 1)
    def _():
        for k, (before, p, q1, q2, q3) in enumerate(sweeps):
            l0 = before.T
            l1 = nn(p, l0, HIGHEST)
            l2 = nn(p, l1, HIGHEST)
            s0, s1, s2 = [nn(a_t, l, HIGHEST) for l in (l0, l1, l2)]
            hi, lo = halves(jnp.concatenate([s0, s1, s2, l0, l1, l2], axis=0))
            lefts[k] = jnp.concatenate([hi, hi, lo], axis=1)
            steps[0, k], steps[1, k] = halves(
                0.25 * jnp.concatenate([q3, -q2, q1, -unit], axis=0)
            )
            sides[0, k], sides[1, k] = halves(
                0.25
                * jnp.concatenate([7.0 * l1 - 15.0 * l0 - l2, 7.0 * l0 - l1, -l0], axis=0)
            )

    wait_bytes(fin.at[0 : CHIPS - 1], e2_r)

    @pl.when(core == 0)
    def _():
        wait_bytes(mt_f.at[0 : CHIPS - 1], e2t_r)
        rows = jnp.concatenate([mt_f[s] for s in range(CHIPS)], axis=0)
        top = jnp.max(rows, axis=0, keepdims=True)
        factor = jnp.exp(rows - top)
        total = jnp.sum(factor * pltpu.roll(rows, M, 1), axis=0, keepdims=True)
        inverse = jnp.where(low, 1.0 / jnp.where(low, total, 1.0), 0.0)
        weight = nt(eye_low, factor * inverse, HIGHEST)
        summed = fin[0] * weight[:, 0:1]
        for s in range(1, CHIPS):
            summed = summed + fin[s] * weight[:, s : s + 1]
        sum_s[...] = summed
        cmat_out[...] = summed
        remote(cmat_out, cmat_in, cm_s, cm_r, partner).start()
        stat[...] = jnp.where(low, top, pltpu.roll(inverse, M, 1))

    @pl.when(core == 1)
    def _():
        summed = fin[0]
        for s in range(1, CHIPS):
            summed = summed + fin[s]
        sum_s[...] = summed

    summed = sum_s[...]
    made = nn(left, summed, HIGHEST).astype(BF)
    res[...] = made
    for dx, dy in STEPS:
        remote(res, ab.at[chip], e3_s, e3_r.at[dx], peer((dx, dy, 1))).start()

    @pl.when(core == 0)
    def _():
        sb[chip] = stat[...]
        for dx, dy in OTHERS:
            remote(stat, sb.at[chip], e3t_s, e3t_r.at[dx], peer((dx, dy, 0))).start()
        wait_bytes(cmat_out, cm_s)

    @pl.when(core == 1)
    def _():
        wait_bytes(cmat_in, cm_r)
        c = cmat_in[...]
        dots = jnp.sum(made.astype(F32) * c, axis=1, keepdims=True)
        stat[...] = jnp.sum(jnp.where(diag_low, dots, 0.0), axis=0, keepdims=True)
        for dx, dy in STEPS:
            remote(stat, sb.at[CHIPS + chip], e3t_s, e3t_r.at[dx], peer((dx, dy, 1))).start()
        grad = nt(summed, c, HIGHEST)
        a_grad = jnp.zeros((M, M), F32)
        for k in range(ITERS - 1, -1, -1):
            hi, lo = halves(grad)
            turned = nn(lefts[k], jnp.concatenate([hi, lo, hi], axis=0))
            parts = [turned[i * M : (i + 1) * M] for i in range(6)]
            grad = by_halves([grad] + parts[:3], steps[0, k], steps[1, k])
            a_grad = a_grad + by_halves(parts[3:], sides[0, k], sides[1, k])
        a_grad = a_grad + grad.T / divisor
        a_score = a * (a_grad - jnp.sum(a * a_grad, axis=1, keepdims=True))
        asc_out[...] = nn(a_score, kl_own, HIGHEST) * SCALE
        remote(asc_out, asc_in, as_s, as_r, partner).start()
        asc_s[...] = nn(a_score.T, ql_own, HIGHEST) * SCALE

    for dx in (0, 1, 3, 2):
        row = lax.rem(x + NX - dx, NX) * NY
        heads = [row + j for j in range(NY)]
        wait_bytes(ab.at[0:NY], e3_r.at[dx])

        @pl.when(core == 0)
        def _():
            wait_bytes(sb.at[0 : (2 * NY - 1 if dx == 0 else 2 * NY)], e3t_r.at[dx])
            alphas = []
            for h in heads:
                both = sb[h]
                shift = jnp.exp(jnp.where(low, mt_s[h] - both, 0.0))
                alphas.append(jnp.where(low, shift * pltpu.roll(both, M, 1), 0.0))
            dots = [sb[CHIPS + h] for h in heads]
            cols = nt(eye_low, jnp.concatenate(alphas + dots, axis=0), HIGHEST)
            grads = [nt(ab[h], b_v[:, head_cols(h)]) for h in heads]
            outs = []
            for j, (h, bg) in enumerate(zip(heads, grads)):
                prob = w_s[h] * cols[:, j : j + 1]
                score = (prob * (bg - cols[:, NY + j : NY + j + 1])).astype(BF)
                outs.append((prob.astype(BF), score, nn(score, a_v[:, head_cols(h)]) * SCALE))
            for h, (prob, score, sums) in zip(heads, outs):
                bl_s[h] = prob
                bs_s[h] = score
                s32[pl.ds(h, M, stride=H), :] = sums

        @pl.when(core == 1)
        def _():
            grads = [nt(ab[h], b_v[:, head_cols(h)]) for h in heads]
            outs = []
            for h, fg in zip(heads, grads):
                prob = w_s[h]
                score = (prob * (fg - jnp.sum(prob * fg, axis=0, keepdims=True))).astype(BF)
                outs.append((prob.astype(BF), score, nn(score, a_v[:, head_cols(h)]) * SCALE))
            for h, (prob, score, sums) in zip(heads, outs):
                bl_s[h] = prob
                bs_s[h] = score
                s32[pl.ds(h, M, stride=H), :] = sums

    @pl.when(core == 0)
    def _():
        wait_bytes(asc_in, as_r)
        asc_s[...] = asc_in[...]

    at_own = pl.ds(chip, M, stride=H)
    s32[at_own, :] = s32[at_own, :] + asc_s[...]
    for d in range(CHIPS):
        for c in range(NC):
            at = (d * NC + c) * 32
            s16[d, c] = s32[at : at + 32, :].astype(BF)
    r4[core * CHIPS + chip] = s16[chip, core]
    for offset in OFFSETS:
        target = peer(offset)
        remote(
            s16.at[target // NC, lax.rem(target, NC)], r4.at[core * CHIPS + chip],
            e4_s, e4_r, target,
        ).start()

    for first in range(0, H, 4):
        for h in range(first, first + 4):
            at = slice(h * DH, (h + 1) * DH)
            part2 = tn(bs_s[h], lm[h]) * SCALE
            part1 = tn(bl_s[h], ab[h]).astype(BF)
            for c in range(NC):
                x2_s[c, :, at] = part2[c * ROWS : (c + 1) * ROWS]
                x1_s[c, :, at] = part1[c * ROWS : (c + 1) * ROWS]
        cols = pl.ds(first * DH, 4 * DH)

        def move(kept1, kept2, given1, given2, c):
            for slot, (src, kept, given) in enumerate(
                ((x1_s, kept1, given1), (x2_s, kept2, given2))
            ):
                remote(
                    src.at[1 - c, :, cols], given.at[:, cols], x_s.at[slot], x_r.at[slot], partner
                ).start()
                pltpu.make_async_copy(
                    src.at[c, :, cols], kept.at[:, cols], x_s.at[2 + slot]
                ).start()

        @pl.when(core == 0)
        def _():
            move(vg_v, kg32, vg_v, kg32, 0)

        @pl.when(core == 1)
        def _():
            move(att_v, qg32, att_v, qg32, 1)

    wait_bytes(r4.at[0 : GROUP - 1], e4_r)
    for c in range(NC):
        total = r4[c * CHIPS].astype(F32)
        for d in range(1, CHIPS):
            total = total + r4[c * CHIPS + d].astype(F32)
        land[c * 32 : (c + 1) * 32, :] = total * (1.0 / SEG)

    for slot, ref in ((0, x1_s), (1, x2_s)):
        wait_bytes(ref.at[0], x_r.at[slot])
        wait_bytes(ref.at[0], x_s.at[slot])
        wait_bytes(ref.at[0], x_s.at[2 + slot])
    for slot, ref in ((0, a_v), (1, b_v)):
        wait_bytes(ref.at[0:ROWS], pre_s.at[slot])
    wait_bytes(rb.at[0 : GROUP - 1], e1_s)
    hand.wait_send()
    wait_bytes(fin.at[0 : CHIPS - 1], e2_s)
    wait_bytes(ab.at[0:CHIPS], e3_s)

    @pl.when(core == 0)
    def _():
        wait_bytes(mt_f.at[0 : CHIPS - 1], e2t_s)
        wait_bytes(sb.at[0 : CHIPS - 1], e3t_s)

    @pl.when(core == 1)
    def _():
        wait_bytes(sb.at[0:CHIPS], e3t_s)
        wait_bytes(asc_out, as_s)

    wait_bytes(r4.at[0 : GROUP - 1], e4_s)


def finish_kernel(att, vg, qg32, kg32, land, att_out, qg_out, kg_out, vg_out, qg, kg, sem):
    copies = []

    def store(src, dst):
        copy = pltpu.make_async_copy(src, dst, sem.at[len(copies)])
        copy.start()
        copies.append(copy)

    store(att, att_out)
    store(vg, vg_out)
    for own, out, made, first in ((qg32, qg_out, qg, 0), (kg32, kg_out, kg, 2 * H)):
        for h in range(H):
            at = slice(h * DH, (h + 1) * DH)
            for seg in range(2):
                here = slice(seg * SEG, (seg + 1) * SEG)
                row = first + seg * H + h
                made[here, at] = (own[here, at] + land[row : row + 1, :]).astype(BF)
        store(made, out)
    for copy in copies:
        copy.wait()


def per_device(queries, keys, values, out_grad):
    shape = (ROWS, WIDTH)
    dma = pltpu.SemaphoreType.DMA
    rows = pltpu.VMEM(shape, BF)
    square = pltpu.VMEM((M, DH), F32)
    scratch = (
        [rows] * 2
        + [pltpu.VMEM((NC * ROWS, WIDTH), BF)] * 2
        + [pltpu.VMEM((2, 32, DH), F32), pltpu.VMEM((2, 32, DH), BF)]
        + [pltpu.VMEM((GROUP, 32, DH), BF), pltpu.VMEM((M * H, DH), F32)]
        + [pltpu.VMEM((H, M, DH), BF), pltpu.VMEM((M, DH), BF)]
        + [pltpu.VMEM((H, M, NC * ROWS), F32)]
        + [pltpu.VMEM((H, M, DH), F32)] * 2
        + [pltpu.VMEM((H, 1, DH), F32)] * 2
        + [square]
        + [pltpu.VMEM((ITERS, 6 * M, 3 * M), BF)]
        + [pltpu.VMEM((2, ITERS, n * M, M), BF) for n in (4, 3)]
        + [pltpu.VMEM((M, DH), BF), pltpu.VMEM((1, DH), F32)]
        + [square] * 2
        + [pltpu.VMEM((CHIPS, M, DH), BF), pltpu.VMEM((GROUP, 1, DH), F32)]
        + [pltpu.VMEM((M * H, DH), F32)]
        + [pltpu.VMEM((CHIPS, NC, 32, DH), BF), pltpu.VMEM((GROUP, 32, DH), BF)]
        + [pltpu.VMEM((H, M, NC * ROWS), BF)] * 2
        + [square] * 3
        + [pltpu.VMEM((NC,) + shape, BF), pltpu.VMEM((NC,) + shape, F32)]
        + [dma((4,)), dma((2,)), dma((2,))]
        + [dma] * 8
        + [dma] * 2
        + [dma, dma((NX,)), dma, dma((NX,))]
        + [dma] * 4
        + [dma((4,)), dma((2,))]
    )
    made = pl.pallas_call(
        kernel,
        out_shape=[pltpu.VMEM(shape, BF)] * 2
        + [pltpu.VMEM(shape, F32)] * 2
        + [pltpu.VMEM((64, DH), F32)],
        in_specs=[pl.BlockSpec(memory_space=pl.ANY)] * 4,
        out_specs=[pl.BlockSpec(memory_space=pltpu.VMEM)] * 5,
        scratch_shapes=scratch,
        compiler_params=pltpu.CompilerParams(
            collective_id=0, has_side_effects=True, vmem_limit_bytes=30 << 20
        ),
    )(*[pltpu.with_memory_space_constraint(a, pltpu.HBM) for a in (queries, keys, values, out_grad)])
    return pl.pallas_call(
        finish_kernel,
        out_shape=[jax.ShapeDtypeStruct(shape, BF)] * 4,
        in_specs=[pl.BlockSpec(memory_space=pltpu.VMEM)] * 5,
        out_specs=[pl.BlockSpec(memory_space=pl.ANY)] * 4,
        scratch_shapes=[rows] * 2 + [dma((4,))],
        compiler_params=pltpu.CompilerParams(vmem_limit_bytes=8 << 20),
    )(*made)


def solution(mesh):
    placed = P(("doc", "ctx"), None)
    return jax.shard_map(
        per_device,
        mesh=mesh,
        in_specs=(placed,) * 4,
        out_specs=(placed,) * 4,
        check_vma=False,
    )
```

```python
import jax
import jax.numpy as jnp
from jax import lax
from jax.experimental import pallas as pl
from jax.experimental.pallas import tpu as pltpu
from jax.sharding import PartitionSpec as P

H = 16
DH = 128
M = 64
ITERS = 6
SCALE = DH ** (-0.5)
MESH = pl.DeviceIdType.MESH
HIGHEST = lax.Precision.HIGHEST
BF = jnp.bfloat16
F32 = jnp.float32
NX, NY, NC = 4, 4, 2
CHIPS = NX * NY
GROUP = CHIPS * NC
ROWS = 128
SEG = 64
WIDTH = H * DH

STEPS = [
    (2, 2), (2, 1), (1, 2), (2, 3), (3, 2), (2, 0), (0, 2), (1, 1),
    (3, 3), (1, 3), (3, 1), (1, 0), (0, 1), (3, 0), (0, 3), (0, 0),
]
OTHERS = STEPS[:-1]
OFFSETS = [(dx, dy, dc) for dx, dy in OTHERS for dc in range(NC)] + [(0, 0, 1)]


def nn(a, b, precision=None):
    return lax.dot_general(
        a, b, (((1,), (0,)), ((), ())), precision=precision, preferred_element_type=F32
    )


def nt(a, b, precision=None):
    return lax.dot_general(
        a, b, (((1,), (1,)), ((), ())), precision=precision, preferred_element_type=F32
    )


def tn(a, b, precision=None):
    return lax.dot_general(
        a, b, (((0,), (0,)), ((), ())), precision=precision, preferred_element_type=F32
    )


def halves(a):
    hi = a.astype(BF)
    return hi, (a - hi.astype(F32)).astype(BF)


def by_halves(blocks, right_hi, right_lo):
    hi, lo = halves(jnp.concatenate(blocks, axis=1))
    return nn(hi, right_hi) + (nn(lo, right_hi) + nn(hi, right_lo))


def iota(shape, dim):
    return lax.broadcasted_iota(jnp.int32, shape, dim)


def wait_bytes(ref, sem):
    pltpu.make_async_copy(ref, ref, sem).wait()


def head_cols(h):
    return pl.ds(pl.multiple_of(h * DH, DH), DH)


def kernel(
    q_hbm, k_hbm, v_hbm, g_hbm,
    att_v, vg_v, qg32, kg32, land,
    q_v, k_v, a_v, b_v,
    msg32, msg16, rb, lf, lm, lm_in,
    w_s, part, fin, mt_s, mt_f, sum_s,
    lefts, steps, sides,
    res, stat, cmat_in, cmat_out, ab, sb,
    s32, s16, r4, bs_s, bl_s, asc_out, asc_in, asc_s, x1_s, x2_s,
    in_sem, pre_s, pre_r, e1_s, e1_r, lm_ss, lm_sr, e2_s, e2_r, e2t_s, e2t_r,
    cm_s, cm_r, e3_s, e3_r, e3t_s, e3t_r, as_s, as_r, e4_s, e4_r, x_s, x_r,
):
    me = lax.axis_index("ctx")
    core = lax.rem(me, NC)
    chip = me // NC
    y = lax.rem(chip, NY)
    x = chip // NY
    partner = chip * NC + (1 - core)

    def chip_at(dx, dy):
        return lax.rem(x + dx, NX) * NY + lax.rem(y + dy, NY)

    def peer(offset):
        dx, dy, dc = offset
        return chip_at(dx, dy) * NC + lax.rem(core + dc, NC)

    def remote(src, dst, send, recv, target):
        return pltpu.make_async_remote_copy(
            src_ref=src, dst_ref=dst, send_sem=send, recv_sem=recv,
            device_id={"ctx": target}, device_id_type=MESH,
        )

    barrier = pltpu.get_barrier_semaphore()
    for offset in OFFSETS:
        pl.semaphore_signal(
            barrier, inc=1, device_id={"ctx": peer(offset)}, device_id_type=MESH
        )
    load_q = pltpu.make_async_copy(q_hbm, q_v, in_sem.at[0])
    load_k = pltpu.make_async_copy(k_hbm, k_v, in_sem.at[1])
    load_q.start()
    load_k.start()
    mine = pl.ds(pl.multiple_of(core * ROWS, ROWS), ROWS)

    @pl.when(core == 0)
    def _():
        pltpu.make_async_copy(k_hbm, a_v.at[0:ROWS], in_sem.at[2]).start()
        pltpu.make_async_copy(v_hbm, b_v.at[0:ROWS], in_sem.at[3]).start()

    @pl.when(core == 1)
    def _():
        pltpu.make_async_copy(q_hbm, a_v.at[ROWS : 2 * ROWS], in_sem.at[2]).start()
        pltpu.make_async_copy(g_hbm, b_v.at[ROWS : 2 * ROWS], in_sem.at[3]).start()

    pick = jnp.where(iota((8, ROWS), 0) == iota((8, ROWS), 1) // SEG, 1.0, 0.0).astype(BF)
    for which, load, ref in ((0, load_q, q_v), (1, load_k, k_v)):
        load.wait()
        sums = nn(pick, ref[...]) * (1.0 / SEG)
        for seg in range(2):
            for h in range(H):
                row = seg * H + h
                msg32[which, row : row + 1, :] = sums[seg : seg + 1, h * DH : (h + 1) * DH]
    msg16[...] = msg32[...].astype(BF)
    rb[me] = msg16[core]
    pl.semaphore_wait(barrier, GROUP - 1)
    for offset in OFFSETS:
        target = peer(offset)
        remote(msg16.at[lax.rem(target, NC)], rb.at[me], e1_s, e1_r, target).start()

    @pl.when(core == 0)
    def _():
        remote(q_hbm, a_v.at[0:ROWS], pre_s.at[0], pre_r.at[0], partner).start()
        remote(g_hbm, b_v.at[0:ROWS], pre_s.at[1], pre_r.at[1], partner).start()

    @pl.when(core == 1)
    def _():
        remote(k_hbm, a_v.at[ROWS : 2 * ROWS], pre_s.at[0], pre_r.at[0], partner).start()
        remote(v_hbm, b_v.at[ROWS : 2 * ROWS], pre_s.at[1], pre_r.at[1], partner).start()

    wait_bytes(a_v.at[mine], in_sem.at[2])
    wait_bytes(b_v.at[mine], in_sem.at[3])
    for slot, ref in ((0, a_v), (1, b_v)):
        wait_bytes(ref.at[0:ROWS], pre_r.at[slot])
    wait_bytes(rb.at[0 : GROUP - 1], e1_r)
    for d in range(GROUP):
        lf[d * 32 : (d + 1) * 32, :] = rb[d].astype(F32)
    for h in range(H):
        lm[h] = lf[pl.ds(h, M, stride=H), :].astype(BF)
    hand = remote(lm.at[chip], lm_in, lm_ss, lm_sr, partner)
    hand.start()

    row_at = iota((M, DH), 0)
    lane_at = iota((M, DH), 1)
    diag_low = lane_at == row_at
    diag_high = lane_at == row_at + M
    low = iota((1, DH), 1) < M
    eye_low = jnp.where(diag_low, 1.0, 0.0)

    def value_group(heads):
        scores = [nt(lm[h], a_v[:, head_cols(h)]) * SCALE for h in heads]
        outs = []
        for h, s in zip(heads, scores):
            m = jnp.max(s, axis=1, keepdims=True)
            w = jnp.exp(s - m)
            t = jnp.sum(w, axis=1, keepdims=True)
            hi = w.astype(BF)
            lo = (w - hi.astype(F32)).astype(BF)
            vals = b_v[:, head_cols(h)]
            sums = nn(hi, vals) + nn(lo, vals)
            row = jnp.sum(
                jnp.where(diag_low, m, 0.0) + jnp.where(diag_high, t, 0.0), axis=0, keepdims=True
            )
            outs.append((w, sums, row))
        for h, (w, sums, row) in zip(heads, outs):
            w_s[h] = w
            part[h] = sums
            mt_s[h] = row

    def gradient_group(heads):
        scores = [nt(lm[h], a_v[:, head_cols(h)]) * SCALE for h in heads]
        outs = []
        for h, s in zip(heads, scores):
            e = jnp.exp(s - jnp.max(s, axis=0, keepdims=True))
            prob = e / jnp.sum(e, axis=0, keepdims=True)
            outs.append((prob, nn(prob.astype(BF), b_v[:, head_cols(h)])))
        for h, (prob, sums) in zip(heads, outs):
            w_s[h] = prob
            part[h] = sums

    for i in range(NX):
        group = STEPS[i * NY : (i + 1) * NY]
        heads = [chip_at(*step) for step in group]

        @pl.when(core == 0)
        def _():
            value_group(heads)
            for step, h in zip(group, heads):
                if step == (0, 0):
                    mt_f[chip] = mt_s[h]
                else:
                    remote(mt_s.at[h], mt_f.at[chip], e2t_s, e2t_r, h * NC).start()

        @pl.when(core == 1)
        def _():
            gradient_group(heads)

        for step, h in zip(group, heads):
            if step == (0, 0):
                fin[chip] = part[h]
            else:
                remote(part.at[h], fin.at[chip], e2_s, e2_r, h * NC + core).start()

    hand.wait_recv()
    own = lm[chip].astype(F32)
    other = lm_in[...].astype(F32)
    ql_own = jnp.where(core == 0, own, other)
    kl_own = jnp.where(core == 0, other, own)
    scores = nt(ql_own.astype(BF), kl_own.astype(BF)) * SCALE
    e = jnp.exp(scores - jnp.max(scores, axis=1, keepdims=True))
    a = e / jnp.sum(e, axis=1, keepdims=True)
    divisor = jnp.max(jnp.sum(a, axis=0, keepdims=True), axis=1, keepdims=True) * jnp.max(
        jnp.sum(a, axis=1, keepdims=True), axis=0, keepdims=True
    )
    a_t = a.T
    z = a_t / divisor
    unit = jnp.where(iota((M, M), 0) == iota((M, M), 1), 1.0, 0.0)
    sweeps = []
    for _ in range(ITERS):
        p = nn(a, z, HIGHEST)
        q1 = 7.0 * unit - p
        q2 = 15.0 * unit - nn(p, q1, HIGHEST)
        q3 = 13.0 * unit - nn(p, q2, HIGHEST)
        sweeps.append((z, p, q1, q2, q3))
        z = 0.25 * nn(z, q3, HIGHEST)
    left = jnp.where(core == 0, z, z.T)

    @pl.when(core == 1)
    def _():
        for k, (before, p, q1, q2, q3) in enumerate(sweeps):
            l0 = before.T
            l1 = nn(p, l0, HIGHEST)
            l2 = nn(p, l1, HIGHEST)
            s0, s1, s2 = [nn(a_t, l, HIGHEST) for l in (l0, l1, l2)]
            hi, lo = halves(jnp.concatenate([s0, s1, s2, l0, l1, l2], axis=0))
            lefts[k] = jnp.concatenate([hi, hi, lo], axis=1)
            steps[0, k], steps[1, k] = halves(
                0.25 * jnp.concatenate([q3, -q2, q1, -unit], axis=0)
            )
            sides[0, k], sides[1, k] = halves(
                0.25
                * jnp.concatenate([7.0 * l1 - 15.0 * l0 - l2, 7.0 * l0 - l1, -l0], axis=0)
            )

    wait_bytes(fin.at[0 : CHIPS - 1], e2_r)

    @pl.when(core == 0)
    def _():
        wait_bytes(mt_f.at[0 : CHIPS - 1], e2t_r)
        rows = jnp.concatenate([mt_f[s] for s in range(CHIPS)], axis=0)
        top = jnp.max(rows, axis=0, keepdims=True)
        factor = jnp.exp(rows - top)
        total = jnp.sum(factor * pltpu.roll(rows, M, 1), axis=0, keepdims=True)
        inverse = jnp.where(low, 1.0 / jnp.where(low, total, 1.0), 0.0)
        weight = nt(eye_low, factor * inverse, HIGHEST)
        summed = fin[0] * weight[:, 0:1]
        for s in range(1, CHIPS):
            summed = summed + fin[s] * weight[:, s : s + 1]
        sum_s[...] = summed
        cmat_out[...] = summed
        remote(cmat_out, cmat_in, cm_s, cm_r, partner).start()
        stat[...] = jnp.where(low, top, pltpu.roll(inverse, M, 1))

    @pl.when(core == 1)
    def _():
        summed = fin[0]
        for s in range(1, CHIPS):
            summed = summed + fin[s]
        sum_s[...] = summed

    summed = sum_s[...]
    made = nn(left, summed, HIGHEST).astype(BF)
    res[...] = made
    for dx, dy in STEPS:
        remote(res, ab.at[chip], e3_s, e3_r.at[dx], peer((dx, dy, 1))).start()

    @pl.when(core == 0)
    def _():
        sb[chip] = stat[...]
        for dx, dy in OTHERS:
            remote(stat, sb.at[chip], e3t_s, e3t_r.at[dx], peer((dx, dy, 0))).start()
        wait_bytes(cmat_out, cm_s)

    @pl.when(core == 1)
    def _():
        wait_bytes(cmat_in, cm_r)
        c = cmat_in[...]
        dots = jnp.sum(made.astype(F32) * c, axis=1, keepdims=True)
        stat[...] = jnp.sum(jnp.where(diag_low, dots, 0.0), axis=0, keepdims=True)
        for dx, dy in STEPS:
            remote(stat, sb.at[CHIPS + chip], e3t_s, e3t_r.at[dx], peer((dx, dy, 1))).start()
        grad = nt(summed, c, HIGHEST)
        a_grad = jnp.zeros((M, M), F32)
        for k in range(ITERS - 1, -1, -1):
            hi, lo = halves(grad)
            turned = nn(lefts[k], jnp.concatenate([hi, lo, hi], axis=0))
            parts = [turned[i * M : (i + 1) * M] for i in range(6)]
            grad = by_halves([grad] + parts[:3], steps[0, k], steps[1, k])
            a_grad = a_grad + by_halves(parts[3:], sides[0, k], sides[1, k])
        a_grad = a_grad + grad.T / divisor
        a_score = a * (a_grad - jnp.sum(a * a_grad, axis=1, keepdims=True))
        asc_out[...] = nn(a_score, kl_own, HIGHEST) * SCALE
        remote(asc_out, asc_in, as_s, as_r, partner).start()
        asc_s[...] = nn(a_score.T, ql_own, HIGHEST) * SCALE

    for dx in (0, 1, 3, 2):
        row = lax.rem(x + NX - dx, NX) * NY
        heads = [row + j for j in range(NY)]
        wait_bytes(ab.at[0:NY], e3_r.at[dx])

        @pl.when(core == 0)
        def _():
            wait_bytes(sb.at[0 : (2 * NY - 1 if dx == 0 else 2 * NY)], e3t_r.at[dx])
            alphas = []
            for h in heads:
                both = sb[h]
                shift = jnp.exp(jnp.where(low, mt_s[h] - both, 0.0))
                alphas.append(jnp.where(low, shift * pltpu.roll(both, M, 1), 0.0))
            dots = [sb[CHIPS + h] for h in heads]
            cols = nt(eye_low, jnp.concatenate(alphas + dots, axis=0), HIGHEST)
            grads = [nt(ab[h], b_v[:, head_cols(h)]) for h in heads]
            outs = []
            for j, (h, bg) in enumerate(zip(heads, grads)):
                prob = w_s[h] * cols[:, j : j + 1]
                score = (prob * (bg - cols[:, NY + j : NY + j + 1])).astype(BF)
                outs.append((prob.astype(BF), score, nn(score, a_v[:, head_cols(h)]) * SCALE))
            for h, (prob, score, sums) in zip(heads, outs):
                bl_s[h] = prob
                bs_s[h] = score
                s32[pl.ds(h, M, stride=H), :] = sums

        @pl.when(core == 1)
        def _():
            grads = [nt(ab[h], b_v[:, head_cols(h)]) for h in heads]
            outs = []
            for h, fg in zip(heads, grads):
                prob = w_s[h]
                score = (prob * (fg - jnp.sum(prob * fg, axis=0, keepdims=True))).astype(BF)
                outs.append((prob.astype(BF), score, nn(score, a_v[:, head_cols(h)]) * SCALE))
            for h, (prob, score, sums) in zip(heads, outs):
                bl_s[h] = prob
                bs_s[h] = score
                s32[pl.ds(h, M, stride=H), :] = sums

    @pl.when(core == 0)
    def _():
        wait_bytes(asc_in, as_r)
        asc_s[...] = asc_in[...]

    at_own = pl.ds(chip, M, stride=H)
    s32[at_own, :] = s32[at_own, :] + asc_s[...]
    r4[core * CHIPS + chip] = s32[pl.ds(pl.multiple_of(me * 32, 32), 32), :].astype(BF)
    for offset in OFFSETS:
        target = peer(offset)
        block = s32[pl.ds(pl.multiple_of(target * 32, 32), 32), :]
        s16[target // NC, lax.rem(target, NC)] = block.astype(BF)
        remote(
            s16.at[target // NC, lax.rem(target, NC)], r4.at[core * CHIPS + chip],
            e4_s, e4_r, target,
        ).start()

    for first in range(0, H, 4):
        for h in range(first, first + 4):
            at = slice(h * DH, (h + 1) * DH)
            part2 = tn(bs_s[h], lm[h]) * SCALE
            part1 = tn(bl_s[h], ab[h]).astype(BF)
            for c in range(NC):
                x2_s[c, :, at] = part2[c * ROWS : (c + 1) * ROWS]
                x1_s[c, :, at] = part1[c * ROWS : (c + 1) * ROWS]
        cols = pl.ds(first * DH, 4 * DH)

        def move(kept1, kept2, given1, given2, c):
            for slot, (src, kept, given) in enumerate(
                ((x1_s, kept1, given1), (x2_s, kept2, given2))
            ):
                remote(
                    src.at[1 - c, :, cols], given.at[:, cols], x_s.at[slot], x_r.at[slot], partner
                ).start()
                pltpu.make_async_copy(
                    src.at[c, :, cols], kept.at[:, cols], x_s.at[2 + slot]
                ).start()

        @pl.when(core == 0)
        def _():
            move(vg_v, kg32, vg_v, kg32, 0)

        @pl.when(core == 1)
        def _():
            move(att_v, qg32, att_v, qg32, 1)

    wait_bytes(r4.at[0 : GROUP - 1], e4_r)
    for c in range(NC):
        total = r4[c * CHIPS].astype(F32)
        for d in range(1, CHIPS):
            total = total + r4[c * CHIPS + d].astype(F32)
        land[c * 32 : (c + 1) * 32, :] = total * (1.0 / SEG)

    for slot, ref in ((0, x1_s), (1, x2_s)):
        wait_bytes(ref.at[0], x_r.at[slot])
        wait_bytes(ref.at[0], x_s.at[slot])
        wait_bytes(ref.at[0], x_s.at[2 + slot])
    for slot, ref in ((0, a_v), (1, b_v)):
        wait_bytes(ref.at[0:ROWS], pre_s.at[slot])
    wait_bytes(rb.at[0 : GROUP - 1], e1_s)
    hand.wait_send()
    wait_bytes(fin.at[0 : CHIPS - 1], e2_s)
    wait_bytes(ab.at[0:CHIPS], e3_s)

    @pl.when(core == 0)
    def _():
        wait_bytes(mt_f.at[0 : CHIPS - 1], e2t_s)
        wait_bytes(sb.at[0 : CHIPS - 1], e3t_s)

    @pl.when(core == 1)
    def _():
        wait_bytes(sb.at[0:CHIPS], e3t_s)
        wait_bytes(asc_out, as_s)

    wait_bytes(r4.at[0 : GROUP - 1], e4_s)


def finish_kernel(att, vg, qg32, kg32, land, att_out, qg_out, kg_out, vg_out, qg, kg, sem):
    copies = []

    def store(src, dst):
        copy = pltpu.make_async_copy(src, dst, sem.at[len(copies)])
        copy.start()
        copies.append(copy)

    store(att, att_out)
    store(vg, vg_out)
    for own, out, made, first in ((qg32, qg_out, qg, 0), (kg32, kg_out, kg, 2 * H)):
        for h in range(H):
            at = slice(h * DH, (h + 1) * DH)
            for seg in range(2):
                here = slice(seg * SEG, (seg + 1) * SEG)
                row = first + seg * H + h
                made[here, at] = (own[here, at] + land[row : row + 1, :]).astype(BF)
            if h % 8 == 7:
                done = pl.ds((h - 7) * DH, 8 * DH)
                store(made.at[:, done], out.at[:, done])
    for copy in copies:
        copy.wait()


def per_device(queries, keys, values, out_grad):
    shape = (ROWS, WIDTH)
    dma = pltpu.SemaphoreType.DMA
    rows = pltpu.VMEM(shape, BF)
    square = pltpu.VMEM((M, DH), F32)
    scratch = (
        [rows] * 2
        + [pltpu.VMEM((NC * ROWS, WIDTH), BF)] * 2
        + [pltpu.VMEM((2, 32, DH), F32), pltpu.VMEM((2, 32, DH), BF)]
        + [pltpu.VMEM((GROUP, 32, DH), BF), pltpu.VMEM((M * H, DH), F32)]
        + [pltpu.VMEM((H, M, DH), BF), pltpu.VMEM((M, DH), BF)]
        + [pltpu.VMEM((H, M, NC * ROWS), F32)]
        + [pltpu.VMEM((H, M, DH), F32)] * 2
        + [pltpu.VMEM((H, 1, DH), F32)] * 2
        + [square]
        + [pltpu.VMEM((ITERS, 6 * M, 3 * M), BF)]
        + [pltpu.VMEM((2, ITERS, n * M, M), BF) for n in (4, 3)]
        + [pltpu.VMEM((M, DH), BF), pltpu.VMEM((1, DH), F32)]
        + [square] * 2
        + [pltpu.VMEM((CHIPS, M, DH), BF), pltpu.VMEM((GROUP, 1, DH), F32)]
        + [pltpu.VMEM((M * H, DH), F32)]
        + [pltpu.VMEM((CHIPS, NC, 32, DH), BF), pltpu.VMEM((GROUP, 32, DH), BF)]
        + [pltpu.VMEM((H, M, NC * ROWS), BF)] * 2
        + [square] * 3
        + [pltpu.VMEM((NC,) + shape, BF), pltpu.VMEM((NC,) + shape, F32)]
        + [dma((4,)), dma((2,)), dma((2,))]
        + [dma] * 8
        + [dma] * 2
        + [dma, dma((NX,)), dma, dma((NX,))]
        + [dma] * 4
        + [dma((4,)), dma((2,))]
    )
    made = pl.pallas_call(
        kernel,
        out_shape=[pltpu.VMEM(shape, BF)] * 2
        + [pltpu.VMEM(shape, F32)] * 2
        + [pltpu.VMEM((64, DH), F32)],
        in_specs=[pl.BlockSpec(memory_space=pl.ANY)] * 4,
        out_specs=[pl.BlockSpec(memory_space=pltpu.VMEM)] * 5,
        scratch_shapes=scratch,
        compiler_params=pltpu.CompilerParams(
            collective_id=0, has_side_effects=True, vmem_limit_bytes=30 << 20
        ),
    )(*[pltpu.with_memory_space_constraint(a, pltpu.HBM) for a in (queries, keys, values, out_grad)])
    return pl.pallas_call(
        finish_kernel,
        out_shape=[jax.ShapeDtypeStruct(shape, BF)] * 4,
        in_specs=[pl.BlockSpec(memory_space=pltpu.VMEM)] * 5,
        out_specs=[pl.BlockSpec(memory_space=pl.ANY)] * 4,
        scratch_shapes=[rows] * 2 + [dma((6,))],
        compiler_params=pltpu.CompilerParams(vmem_limit_bytes=8 << 20),
    )(*made)


def solution(mesh):
    placed = P(("doc", "ctx"), None)
    return jax.shard_map(
        per_device,
        mesh=mesh,
        in_specs=(placed,) * 4,
        out_specs=(placed,) * 4,
        check_vma=False,
    )
```
